128 devices in a mesh: ctx: 16 (over y_hi, z, core), tp: 8 (over y_lo, x).
Axes of the slice: x: 4, y: 4 (y_hi: 2, y_lo: 2; y = y_hi * 2 + y_lo), z: 4, core: 2. Of those that a mesh axis runs over, the one named last changes fastest.
Arguments:
- grad_out: bfloat16 [10240, 4096], P(('ctx', 'tp')), may hold values from -3 to 3
- expert_ids: int32 [10240, 8], P(('ctx', 'tp')), may hold values from 0 to 63, all different within a row; in each aligned block of 80 rows (0 to 79, 80 to 159, ...) at most 12 rows name the same one
- combine: bfloat16 [10240, 8], P(('ctx', 'tp')), may hold values from 0.049804688 to 0.5
- gate_saved: bfloat16 [128, 12, 98304], P(None, None, ('ctx', 'tp')), may hold values from -5 to 5
- up_saved: bfloat16 [128, 12, 98304], P(None, None, ('ctx', 'tp')), may hold values from -5 to 5
- gate_weight: bfloat16 [4096, 98304], P(None, ('ctx', 'tp')), may hold values from -0.09375 to 0.09375
- up_weight: bfloat16 [4096, 98304], P(None, ('ctx', 'tp')), may hold values from -0.09375 to 0.09375
- down_weight: bfloat16 [98304, 4096], P(('ctx', 'tp')), may hold values from -0.15625 to 0.15625
Outputs:
- grad_in: bfloat16 [10240, 4096], P(('ctx', 'tp'))
- grad_combine: bfloat16 [10240, 8], P(('ctx', 'tp'))
The draws below stay inside these ranges and needn't reach their ends.
Inputs may be any that keep to these rules, and one draw needn't show every extreme that they name: `expert_ids`: each row names 8 different experts. The rows of one device name any one expert at most 12 times, a bound that some block reaches.
All inputs are finite; a program needn't handle non-finite values.
Results may differ from the reference program's by a relative error of at most 0.0065.
Values may be sent and summed in bfloat16 or wider, within the bound.
A program may use at most 192 MiB of HBM per device.

```python
import math
import jax
import jax.numpy as jnp
import numpy as np
from jax import lax

D = 4096
FF = 1536
TOP = 8
TOK_DEV = 80
EXPERTS = 64
CAP = 12
TOKENS = 10240
N_CTX = 16
N_TP = 8


def shard_levels(rng, dims, pieces, least, high):
    factor_of, own = 1.0, jax.random.fold_in(rng, 6)
    for axis_at, blocks in pieces:
        steps = jnp.exp(jax.random.uniform(jax.random.fold_in(own, axis_at), (blocks,), jnp.float32, least / len(pieces), high / len(pieces)))
        factor_of = factor_of * jnp.repeat(steps, dims[axis_at] // blocks).reshape([-1 if axis == axis_at else 1 for axis in range(len(dims))])
    return factor_of


def deal_out(own_key, own, number, rows, count, top, most, slope):
    ranking = jax.random.permutation(own_key, count)
    crowded, common = load_shares(count, rows * top, most, slope, True), load_shares(count, rows * top, most, slope, False)
    places = jnp.arange(count)

    def named(sizes, offset_by):
        used = int((sizes > 0).sum())
        fixed = max(1, used // 4)
        moved = fixed + (places - fixed + offset_by * (used - fixed)) % max(1, count - fixed)
        return jnp.zeros((count,), jnp.int32).at[ranking[jnp.where(places < fixed, places, moved)]].set(jnp.asarray(sizes, jnp.int32))

    sizes = jnp.where(number % 4 == 0, named(crowded, number // 4), named(common, number - number // 4 - 1))
    mixed = jax.random.permutation(jax.random.fold_in(own, 3), count)
    source_of, sink = mixed[0:count // 2 * 2:2], mixed[1:count // 2 * 2:2]
    slack = jnp.minimum(sizes[source_of] - 1, most - sizes[sink]) // 2
    slack = jnp.where((source_of == ranking[0]) | (sink == ranking[0]) | (sizes[sink] == 0), 0, jnp.maximum(slack, 0))
    moved = jax.random.randint(jax.random.fold_in(own, 4), (count // 2,), 0, 1 << 20) % (slack + 1)
    sizes = sizes.at[source_of].add(-moved).at[sink].add(moved)
    labels = jnp.searchsorted(jnp.cumsum(sizes), jnp.arange(rows * top), side="right").astype(jnp.int32)
    table = labels.reshape(top, rows).T
    table = table[jax.random.permutation(jax.random.fold_in(own, 1), rows)]
    offset_by = jax.random.randint(jax.random.fold_in(own, 2), (rows, 1), 0, top)
    return jnp.take_along_axis(table, (jnp.arange(top)[None, :] + offset_by) % top, axis=1)


def load_shares(amount, total, limit, lean, full):
    weights = [(1 << 20) // math.isqrt(standing ** lean) + 1 for standing in range(1, amount + 1)]
    largest = limit if full else min(limit, max(-(-total // amount), total * weights[0] // sum(weights)))
    least = 1 if total - largest >= amount - 1 else 0
    given, surplus = [largest] + [least] * (amount - 1), total - largest - least * (amount - 1)
    while surplus > 0:
        free = [i for i in range(1, amount) if given[i] < largest] or [i for i in range(1, amount) if given[i] < limit]
        pool, remaining = sum([weights[i] for i in free]), surplus
        for i in free:
            extra = min(limit - given[i], max(1, remaining * weights[i] // pool), surplus)
            given[i] = given[i] + extra
            surplus = surplus - extra
    return np.array(given)


def gaussian(key, extent, scale, reach, pieces=(), kind=jnp.bfloat16):
    drawn = jax.random.normal(key, extent, jnp.float32) * scale
    if len(pieces) > 0:
        drawn = shard_levels(key, extent, pieces, -0.22, 0.18) * drawn
    return jnp.clip(drawn, min=-reach, max=reach).astype(kind)


def setup_inputs(seed: int = 0) -> dict:
    keys = jax.random.split(jax.random.key(seed), 9)
    grad_out = gaussian(keys[0], (TOKENS, D), 0.5, 3.0, ((0, 128),))
    expert_ids_keys = jax.random.split(jax.random.fold_in(keys[1], 1), TOKENS // TOK_DEV)
    expert_ids_turns = jax.random.permutation(jax.random.fold_in(keys[1], 3), TOKENS // TOK_DEV)
    expert_ids = jax.vmap(lambda own, number: deal_out(jax.random.fold_in(keys[1], 2), own, number, TOK_DEV, EXPERTS, TOP, CAP, 1))(expert_ids_keys, expert_ids_turns).reshape((TOKENS, TOP))
    combine = jnp.clip(jnp.exp(math.log(0.5) - 2.306499 * jax.random.uniform(keys[2], (TOKENS, TOP), jnp.float32) ** shard_levels(keys[2], (TOKENS, TOP), ((0, 128),), -0.2, 0.2)), 0.049804688, 0.5).astype(jnp.bfloat16)
    gate_saved = gaussian(keys[3], (N_CTX * N_TP, CAP, EXPERTS * FF), 1.0, 5.0, ((2, 128),))
    up_saved = gaussian(keys[4], (N_CTX * N_TP, CAP, EXPERTS * FF), 1.0, 5.0, ((2, 128),))
    gate_weight = gaussian(keys[5], (D, EXPERTS * FF), D ** -0.5, 0.09375, ((1, 128),))
    up_weight = gaussian(keys[6], (D, EXPERTS * FF), D ** -0.5, 0.09375, ((1, 128),))
    down_weight = gaussian(keys[7], (EXPERTS * FF, D), FF ** -0.5, 0.15625, ((0, 128),))
    return {"grad_out": grad_out, "expert_ids": expert_ids, "combine": combine, "gate_saved": gate_saved, "up_saved": up_saved, "gate_weight": gate_weight, "up_weight": up_weight, "down_weight": down_weight}


def reference(grad_out, expert_ids, combine, gate_saved, up_saved, gate_weight, up_weight, down_weight):
    sources = N_CTX * N_TP
    half_width = FF // 2
    per_source = TOK_DEV * TOP
    ids = expert_ids.reshape(sources, per_source).astype(jnp.int32)
    one_hot = (ids[:, :, None] == jnp.arange(EXPERTS, dtype=jnp.int32)[None, None, :]).astype(jnp.int32)
    before = jnp.cumsum(one_hot, axis=1) - one_hot
    position = jnp.sum(before * one_hot, axis=2).astype(jnp.int32)
    source_ids = jnp.arange(sources, dtype=jnp.int32)[:, None]
    slot_global = ((ids * sources + source_ids) * CAP + position).reshape(-1).astype(jnp.int32)
    token_ids = (source_ids * TOK_DEV + jnp.arange(per_source, dtype=jnp.int32)[None, :] // TOP).reshape(-1)
    total_slots = EXPERTS * sources * CAP
    token_table = jnp.zeros((total_slots,), jnp.int32).at[slot_global].set(token_ids.astype(jnp.int32))
    weight_table = jnp.zeros((total_slots,), jnp.bfloat16).at[slot_global].set(combine.reshape(-1))
    rows = sources * CAP

    def expert_work(expert):
        base = (expert * rows).astype(jnp.int32)
        token_rows = lax.dynamic_slice(token_table, (base,), (rows,))
        grad_rows = grad_out[token_rows]
        weight_rows = lax.dynamic_slice(weight_table, (base,), (rows,)).astype(jnp.float32)[:, None]
        partials = []
        combs = []
        for which in range(2):
            start = (expert * FF + which * half_width).astype(jnp.int32)
            gate_pre = lax.dynamic_slice_in_dim(gate_saved, start, half_width, 2).reshape(rows, half_width).astype(jnp.float32)
            up_vals = lax.dynamic_slice_in_dim(up_saved, start, half_width, 2).reshape(rows, half_width).astype(jnp.float32)
            w_gate = lax.dynamic_slice_in_dim(gate_weight, start, half_width, 1)
            w_up = lax.dynamic_slice_in_dim(up_weight, start, half_width, 1)
            w_down = lax.dynamic_slice_in_dim(down_weight, start, half_width, 0)
            hidden_grad = jnp.dot(grad_rows, w_down.T, preferred_element_type=jnp.float32)
            sigmoid_g = jax.nn.sigmoid(gate_pre)
            activated = gate_pre * sigmoid_g
            combs.append(jnp.sum(activated * up_vals * hidden_grad, axis=1).astype(jnp.bfloat16))
            weighted = hidden_grad * weight_rows
            dgate = (weighted * up_vals * sigmoid_g * (1.0 + gate_pre * (1.0 - sigmoid_g))).astype(jnp.bfloat16)
            dup = (weighted * activated).astype(jnp.bfloat16)
            part = jnp.dot(dgate, w_gate.T, preferred_element_type=jnp.float32) + jnp.dot(dup, w_up.T, preferred_element_type=jnp.float32)
            partials.append(part.astype(jnp.bfloat16))
        row_grad = (partials[0].astype(jnp.float32) + partials[1].astype(jnp.float32)).astype(jnp.bfloat16)
        row_comb = (combs[0].astype(jnp.float32) + combs[1].astype(jnp.float32)).astype(jnp.bfloat16)
        return row_grad, row_comb

    results, comb_results = lax.map(expert_work, jnp.arange(EXPERTS, dtype=jnp.int32))
    picked = results.reshape(total_slots, D)[slot_global]
    grad_in = jnp.sum(picked.astype(jnp.float32).reshape(TOKENS, TOP, D), axis=1).astype(jnp.bfloat16)
    grad_combine = comb_results.reshape(-1)[slot_global].reshape(TOKENS, TOP)
    return grad_in, grad_combine
```

```python
import functools

import jax
import jax.numpy as jnp
from jax import lax
from jax.experimental import pallas as pl
from jax.experimental.pallas import tpu as pltpu
from jax.sharding import PartitionSpec as P

MESH = pl.DeviceIdType.MESH
FLIPS = (0, 1, 2, 4, 3, 5, 6, 7)
BF = jnp.bfloat16
F32 = jnp.float32
NT = (((1,), (1,)), ((), ()))


def bits(f):
    return f & 1, (f >> 1) & 1, (f >> 2) & 1


def outer(v, c):
    return (v + 3 + 2 * ((v + c) % 2)) % 4


def inner(v, c):
    return (v + 1 + 2 * ((v + c) % 2)) % 4


def flipped(xyz, f, c, how):
    return tuple(how(v, c) if b else v for v, b in zip(xyz, bits(f)))


def device(xyz, c):
    x, y, z = xyz
    return ((y // 2 * 4 + z) * 2 + c, (y % 2) * 4 + x)


def expert_of(xyz, c):
    ctx, tp = device(xyz, c)
    return ctx * 4 + tp // 2


def iota(shape, dim):
    return lax.broadcasted_iota(jnp.int32, shape, dim).astype(F32)


def kernel(
    tokens, slots, width, hidden,
    grad_ref, ids_ref, comb_ref, gate_hbm, up_hbm, gw_hbm, uw_hbm, dw_hbm,
    out_ref, outc_ref, recv, ret,
    tok, stage, gw, uw, dw, sav_g, sav_u, gf, uf, dg, du, cacc, gb, rc, sel, selp, selw, plac, wplac, part,
    w_sem, s_sem, l_sem, tok_send, tok_recv, dis_send, dis_recv, ret_send, ret_recv, part_send, part_recv,
):
    ext = 128
    full = width + ext
    half = 4 * slots
    msg = 2 * half
    cover = 16 * half
    ctx, tp = lax.axis_index("ctx"), lax.axis_index("tp")
    c = ctx % 2
    me = (tp % 4, ctx // 8 * 2 + tp // 4, ctx // 2 % 4)
    mbit = tuple((v + c) % 2 for v in me)
    mine = mbit[2] * 4 + mbit[1] * 2 + mbit[0]
    my_expert = expert_of(me, c)

    def member(r):
        b = tuple(1 - v if t else v for v, t in zip(mbit, bits(r)))
        return b[2] * 4 + b[1] * 2 + b[0]

    def rows(start, size):
        return pl.ds(pl.multiple_of(start, 16), size)

    w_copies = [
        pltpu.make_async_copy(a, b, w_sem.at[i])
        for i, (a, b) in enumerate(((dw_hbm, dw), (gw_hbm, gw), (uw_hbm, uw)))
    ]
    for copy in w_copies:
        copy.start()

    def saved_copies(k, q, m):
        p, sc = 2 * k + q // 2, q % 2
        sender = flipped(me, FLIPS[p], sc, outer)
        mb = (m % 2, m // 2 % 2, m // 4)
        src = tuple((v - (v + sc) % 2 + b + 4) % 4 for v, b in zip(sender, mb))
        sctx, stp = device(src, sc)
        s = sctx * 8 + stp
        at = q * 8 + m
        return (
            pltpu.make_async_copy(gate_hbm.at[s], sav_g.at[at], s_sem.at[0, at]),
            pltpu.make_async_copy(up_hbm.at[s], sav_u.at[at], s_sem.at[1, at]),
        )

    def saved_start(k):
        for q in range(4):
            @pl.loop(0, 8)
            def _(m):
                for copy in saved_copies(k, q, m):
                    copy.start()

    def saved_wait(k):
        for q in range(4):
            @pl.loop(0, 8)
            def _(m):
                for copy in saved_copies(k, q, m):
                    copy.wait()

    saved_start(0)

    barrier = pltpu.get_barrier_semaphore()
    friends = [device(me, 1 - c)]
    for f in range(1, 8):
        friends.append(device(flipped(me, f, c, outer), c))
        friends.append(device(flipped(me, f, c, outer), 1 - c))
        friends.append(device(flipped(me, f, 1 - c, outer), 1 - c))
        friends.append(device(flipped(me, f, c, inner), c))
    for friend in friends:
        pl.semaphore_signal(barrier, inc=1, device_id=friend, device_id_type=MESH)

    own = rows(mine * tokens, tokens)
    tok[own, 0:width] = grad_ref[...]
    lane = lax.broadcasted_iota(jnp.int32, (tokens, ext), 1)
    lane64 = jnp.where(lane >= 64, lane - 64, lane)
    ids = ids_ref[...]
    combine = comb_ref[...].astype(F32)
    hot = jnp.zeros((tokens, ext), F32)
    weight = jnp.zeros((tokens, ext), F32)
    for k in range(ids.shape[1]):
        same = ids[:, k : k + 1] == lane64
        hot = jnp.where(same, 1.0, hot)
        weight = jnp.where(same, combine[:, k : k + 1], weight)
    lower = (iota((tokens, tokens), 1) < iota((tokens, tokens), 0)).astype(F32).astype(BF)
    count = jnp.dot(lower, hot.astype(BF), preferred_element_type=F32)
    table = jnp.where(lane < 64, jnp.where(hot > 0.5, count, -1.0), weight)
    tok[own, width:full] = table.astype(BF)

    pl.semaphore_wait(barrier, len(friends))

    def tok_copy(r):
        return pltpu.make_async_remote_copy(
            src_ref=tok.at[own],
            dst_ref=tok.at[own],
            send_sem=tok_send.at[r],
            recv_sem=tok_recv.at[r],
            device_id=device(flipped(me, r, c, inner), c),
            device_id_type=MESH,
        )

    def tok_arrival(r):
        there = rows(member(r) * tokens, tokens)
        return pltpu.make_async_remote_copy(
            src_ref=tok.at[there],
            dst_ref=tok.at[there],
            send_sem=tok_send.at[r],
            recv_sem=tok_recv.at[r],
            device_id=device(flipped(me, r, c, inner), c),
            device_id_type=MESH,
        )

    for r in range(1, 8):
        tok_copy(r).start()

    slane = lax.broadcasted_iota(jnp.int32, (half, ext), 1)
    for i in range(16):
        e = expert_of(flipped(me, FLIPS[i // 2], c, outer), i % 2)
        selp[i * half : (i + 1) * half, :] = jnp.where(slane == e, 1.0, 0.0).astype(BF)
        selw[i * half : (i + 1) * half, :] = jnp.where(slane == e + 64, 1.0, 0.0).astype(BF)

    def slot_of(j):
        block = jnp.floor((j + 0.5) * (1.0 / slots))
        group = jnp.floor((block + 0.5) * 0.25)
        return j - block * slots, block - group * 4

    def owner_of(t):
        return jnp.floor((t + 0.5) * (1.0 / tokens))

    def dis_copy(i, h, p, dc):
        here = rows(i * msg + h * half, half)
        there = rows((2 * p + c) * msg + h * half, half)
        dst = device(flipped(me, FLIPS[p], c, outer), dc)
        return pltpu.make_async_remote_copy(
            src_ref=stage.at[here, pl.ds(0, width)],
            dst_ref=recv.at[there],
            send_sem=dis_send.at[i * 2 + h],
            recv_sem=dis_recv.at[(2 * p + c) * 2 + h],
            device_id=dst,
            device_id_type=MESH,
        )

    def dis_self(h):
        here = rows(c * msg + h * half, half)
        return pltpu.make_async_copy(stage.at[here, pl.ds(0, width)], recv.at[here], l_sem.at[h])

    def dis_arrival(j, h):
        here = rows(j * msg + h * half, half)
        return pltpu.make_async_remote_copy(
            src_ref=stage.at[here, pl.ds(0, width)],
            dst_ref=recv.at[here],
            send_sem=dis_send.at[j * 2 + h],
            recv_sem=dis_recv.at[j * 2 + h],
            device_id=device(me, 1 - c),
            device_id_type=MESH,
        )

    for step in range(2):
        h = mbit[2] if step == 0 else 1 - mbit[2]
        for r in range(4 * step, 4 * step + 4):
            if r > 0:
                tok_arrival(r).wait_recv()
        there = rows(h * 4 * tokens, 4 * tokens)
        tables = tok[there, width:full]
        pos = lax.dot_general(selp[...], tables, NT, preferred_element_type=F32)
        slot, four = slot_of(iota((cover, 1), 0))
        owner = owner_of(iota((1, 4 * tokens), 1))
        sel[...] = jnp.where((pos == slot) & (four == owner), 1.0, 0.0).astype(BF)

        tile = 512

        @pl.loop(0, width // tile)
        def _(n):
            cols = pl.ds(pl.multiple_of(n * tile, tile), tile)
            got = jnp.dot(sel[...], tok[there, cols], preferred_element_type=F32).astype(BF)
            for i in range(16):
                stage[rows(i * msg + h * half, half), cols] = got[i * half : (i + 1) * half]

        dis_self(h).start()
        dis_copy(1 - c, h, 0, 1 - c).start()
        for p in range(1, 8):
            for dc in range(2):
                dis_copy(2 * p + dc, h, p, dc).start()

    slot, four = slot_of(iota((1, cover), 1))
    owner = owner_of(iota((4 * tokens, 1), 0))
    for h in range(2):
        tables = tok[h * 4 * tokens : (h + 1) * 4 * tokens, width:full]
        pos = lax.dot_general(tables, selp[...], NT, preferred_element_type=F32)
        wgt = lax.dot_general(tables, selw[...], NT, preferred_element_type=F32)
        hit = (pos == slot) & (four == owner)
        plac[h] = jnp.where(hit, 1.0, 0.0).astype(BF)
        wplac[h] = jnp.where(hit, wgt, 0.0).astype(BF)

    for copy in w_copies:
        copy.wait()

    def ret_copy(j, h, p, dc):
        here = rows(j * msg + h * half, half)
        there = rows((2 * p + c) * half, half)
        return pltpu.make_async_remote_copy(
            src_ref=stage.at[here],
            dst_ref=ret.at[h, there],
            send_sem=ret_send.at[j * 2 + h],
            recv_sem=ret_recv.at[(2 * p + c) * 2 + h],
            device_id=device(flipped(me, FLIPS[p], dc, outer), dc),
            device_id_type=MESH,
        )

    def ret_self(h):
        here = rows(c * msg + h * half, half)
        return pltpu.make_async_copy(stage.at[here], ret.at[h, rows(c * half, half)], l_sem.at[2 + h])

    def ret_arrival(j, h):
        return pltpu.make_async_remote_copy(
            src_ref=stage.at[rows(j * msg + h * half, half)],
            dst_ref=ret.at[h, rows(j * half, half)],
            send_sem=ret_send.at[j * 2 + h],
            recv_sem=ret_recv.at[j * 2 + h],
            device_id=device(me, 1 - c),
            device_id_type=MESH,
        )

    batch = 4 * msg
    elane = lax.broadcasted_iota(jnp.int32, (batch, ext), 1)
    for k in range(4):
        saved_wait(k)

        @pl.loop(0, 16)
        def _(i):
            pair = pl.ds(pl.multiple_of(i * 2 * slots, 8), 2 * slots)
            for src, dst in ((sav_g, gf), (sav_u, uf)):
                dst[pair, :] = jnp.concatenate(
                    [src[2 * i].astype(F32), src[2 * i + 1].astype(F32)], axis=0
                )

        if k < 3:
            saved_start(k + 1)
        for j in range(4 * k, 4 * k + 4):
            if j >= 2:
                for h in range(2):
                    dis_arrival(j, h).wait_recv()
        if k == 0:
            for h in range(2):
                dis_arrival(1 - c, h).wait_recv()
                dis_self(h).wait()
        buf = gb.at[pl.ds((k % 2) * batch, batch)]
        load = pltpu.make_async_copy(recv.at[pl.ds(k * batch, batch)], buf, l_sem.at[4])
        load.start()
        load.wait()

        cacc[...] = jnp.zeros_like(cacc)
        tile = 256

        @pl.loop(0, hidden // tile)
        def _(n):
            cols = pl.ds(pl.multiple_of(n * tile, tile), tile)
            dh = lax.dot_general(buf[...], dw[cols, :], NT, preferred_element_type=F32)
            g, u = gf[:, cols], uf[:, cols]
            sg = jax.nn.sigmoid(g)
            a = g * sg
            prod = a * u * dh
            total = cacc[...]
            for b in range(tile // ext):
                total = total + prod[:, b * ext : (b + 1) * ext]
            cacc[...] = total
            dg[:, cols] = (dh * u * sg * (1.0 + g * (1.0 - sg))).astype(BF)
            du[:, cols] = (dh * a).astype(BF)

        for j in range(4 * k, 4 * k + 4):
            if j >= 2:
                for h in range(2):
                    dis_copy(j, h, j // 2, j % 2).wait_send()
        if k == 0:
            for h in range(2):
                dis_copy(1 - c, h, 0, 1 - c).wait_send()

        here = pl.ds(k * batch, batch)
        comb = jnp.sum(cacc[...], axis=1, keepdims=True)
        stage[here, width:full] = jnp.where(elane == my_expert, comb, 0.0).astype(BF)
        xtile = 512

        @pl.loop(0, width // xtile)
        def _(n):
            cols = pl.ds(pl.multiple_of(n * xtile, xtile), xtile)
            x = lax.dot_general(dg[...], gw[cols, :], NT, preferred_element_type=F32)
            x = x + lax.dot_general(du[...], uw[cols, :], NT, preferred_element_type=F32)
            stage[here, cols] = x.astype(BF)

        if k == 0:
            for h in range(2):
                ret_self(h).start()
                ret_copy(1 - c, h, 0, 1 - c).start()
        for j in range(4 * k, 4 * k + 4):
            if j >= 2:
                for h in range(2):
                    ret_copy(j, h, j // 2, j % 2).start()

    for r in range(1, 8):
        tok_copy(r).wait_send()

    def part_copy(r):
        return pltpu.make_async_remote_copy(
            src_ref=tok.at[rows(member(r) * tokens, tokens)],
            dst_ref=part.at[pl.ds(r * tokens, tokens)],
            send_sem=part_send.at[r],
            recv_sem=part_recv.at[r],
            device_id=device(flipped(me, r, c, inner), c),
            device_id_type=MESH,
        )

    for step in range(2):
        h = 1 - mbit[2] if step == 0 else mbit[2]
        for j in range(2, 16):
            ret_arrival(j, h).wait_recv()
        ret_arrival(1 - c, h).wait_recv()
        ret_self(h).wait()
        loads = (
            pltpu.make_async_copy(ret.at[h, :, pl.ds(0, width)], gb, l_sem.at[5]),
            pltpu.make_async_copy(ret.at[h, :, pl.ds(width, ext)], rc, l_sem.at[6]),
        )
        for load in loads:
            load.start()
        for load in loads:
            load.wait()
        there = rows(h * 4 * tokens, 4 * tokens)
        tok[there, width:full] = jnp.dot(plac[h], rc[...], preferred_element_type=F32).astype(BF)
        tile = 512

        @pl.loop(0, width // tile)
        def _(n):
            cols = pl.ds(pl.multiple_of(n * tile, tile), tile)
            tok[there, cols] = jnp.dot(wplac[h], gb[:, cols], preferred_element_type=F32).astype(BF)

        for r in range(4 - 4 * step, 8 - 4 * step):
            if r > 0:
                part_copy(r).start()

    for r in range(1, 8):
        part_copy(r).wait_recv()
    tile = 512

    @pl.loop(0, width // tile)
    def _(n):
        cols = pl.ds(pl.multiple_of(n * tile, tile), tile)
        total = tok[own, cols].astype(F32)
        for r in range(1, 8):
            total = total + part[r * tokens : (r + 1) * tokens, cols].astype(F32)
        out_ref[:, cols] = total.astype(BF)

    total = tok[own, width:full].astype(F32)
    for r in range(1, 8):
        total = total + part[r * tokens : (r + 1) * tokens, width:full].astype(F32)
    total = jnp.where(lane < 64, total, 0.0)
    klane = lax.broadcasted_iota(jnp.int32, ids.shape, 1)
    result = jnp.zeros(ids.shape, F32)
    for k in range(ids.shape[1]):
        value = jnp.sum(jnp.where(ids[:, k : k + 1] == lane, total, 0.0), axis=1, keepdims=True)
        result = jnp.where(klane == k, value, result)
    outc_ref[...] = result.astype(BF)

    for r in range(1, 8):
        part_copy(r).wait_send()
    for h in range(2):
        ret_copy(1 - c, h, 0, 1 - c).wait_send()
        for j in range(2, 16):
            ret_copy(j, h, j // 2, j % 2).wait_send()


def body(grad_out, expert_ids, combine, gate_saved, up_saved, gate_weight, up_weight, down_weight):
    tokens, width = grad_out.shape
    sources, slots, hidden = gate_saved.shape
    top = expert_ids.shape[1]
    full = width + 128
    half = 4 * slots
    cover = 16 * half
    batch = 8 * half
    vmem = pl.BlockSpec(memory_space=pltpu.VMEM)
    hbm = pl.BlockSpec(memory_space=pl.ANY)
    dma = pltpu.SemaphoreType.DMA
    out = pl.pallas_call(
        functools.partial(kernel, tokens, slots, width, hidden),
        out_shape=(
            jax.ShapeDtypeStruct((tokens, width), BF),
            jax.ShapeDtypeStruct((tokens, top), BF),
            jax.ShapeDtypeStruct((2 * cover, width), BF),
            jax.ShapeDtypeStruct((2, cover, full), BF),
        ),
        in_specs=[vmem, vmem, vmem, hbm, hbm, hbm, hbm, hbm],
        out_specs=(vmem, vmem, hbm, hbm),
        scratch_shapes=[
            pltpu.VMEM((8 * tokens, full), BF),
            pltpu.VMEM((2 * cover, full), BF),
            pltpu.VMEM((width, hidden), BF),
            pltpu.VMEM((width, hidden), BF),
            pltpu.VMEM((hidden, width), BF),
            pltpu.VMEM((32, slots, hidden), BF),
            pltpu.VMEM((32, slots, hidden), BF),
            pltpu.VMEM((batch, hidden), F32),
            pltpu.VMEM((batch, hidden), F32),
            pltpu.VMEM((batch, hidden), BF),
            pltpu.VMEM((batch, hidden), BF),
            pltpu.VMEM((batch, 128), F32),
            pltpu.VMEM((cover, width), BF),
            pltpu.VMEM((cover, 128), BF),
            pltpu.VMEM((cover, 4 * tokens), BF),
            pltpu.VMEM((cover, 128), BF),
            pltpu.VMEM((cover, 128), BF),
            pltpu.VMEM((2, 4 * tokens, cover), BF),
            pltpu.VMEM((2, 4 * tokens, cover), BF),
            pltpu.VMEM((8 * tokens, full), BF),
            dma((3,)),
            dma((2, 32)),
            dma((7,)),
            dma((8,)),
            dma((8,)),
            dma((32,)),
            dma((32,)),
            dma((32,)),
            dma((32,)),
            dma((8,)),
            dma((8,)),
        ],
        compiler_params=pltpu.CompilerParams(
            collective_id=0, has_side_effects=True, vmem_limit_bytes=66 * 1000 * 1000
        ),
        cost_estimate=pl.CostEstimate(
            flops=6 * sources * slots * hidden * width,
            bytes_accessed=80_000_000,
            transcendentals=sources * slots * hidden,
        ),
    )(grad_out, expert_ids, combine, gate_saved, up_saved, gate_weight, up_weight, down_weight)
    return out[0], out[1]


def solution(mesh):
    placed = (
        P(("ctx", "tp"), None),
        P(("ctx", "tp"), None),
        P(("ctx", "tp"), None),
        P(None, None, ("ctx", "tp")),
        P(None, None, ("ctx", "tp")),
        P(None, ("ctx", "tp")),
        P(None, ("ctx", "tp")),
        P(("ctx", "tp"), None),
    )
    return jax.shard_map(
        body,
        mesh=mesh,
        in_specs=placed,
        out_specs=(P(("ctx", "tp"), None), P(("ctx", "tp"), None)),
        check_vma=False,
    )
```

```python
import functools

import jax
import jax.numpy as jnp
from jax import lax
from jax.experimental import pallas as pl
from jax.experimental.pallas import tpu as pltpu
from jax.sharding import PartitionSpec as P

MESH = pl.DeviceIdType.MESH
FLIPS = (0, 7, 1, 6, 2, 5, 3, 4)
BF = jnp.bfloat16
F32 = jnp.float32
NT = (((1,), (1,)), ((), ()))


def bits(f):
    return f & 1, (f >> 1) & 1, (f >> 2) & 1


def outer(v, c):
    return (v + 3 + 2 * ((v + c) % 2)) % 4


def inner(v, c):
    return (v + 1 + 2 * ((v + c) % 2)) % 4


def flipped(xyz, f, c, how):
    return tuple(how(v, c) if b else v for v, b in zip(xyz, bits(f)))


def device(xyz, c):
    x, y, z = xyz
    return ((y // 2 * 4 + z) * 2 + c, (y % 2) * 4 + x)


def expert_of(xyz, c):
    ctx, tp = device(xyz, c)
    return ctx * 4 + tp // 2


def iota(shape, dim):
    return lax.broadcasted_iota(jnp.int32, shape, dim).astype(F32)


def kernel(
    tokens, slots, width, hidden,
    grad_ref, ids_ref, comb_ref, gate_hbm, up_hbm, gw_hbm, uw_hbm, dw_hbm,
    out_ref, outc_ref, recv, ret,
    tok, stage, gw, uw, dw, sav_g, sav_u, gf, uf, dg, du, perm, cacc, gb, rc, sel, selp, selw, plac, wplac, part,
    w_sem, l_sem, tok_send, tok_recv, dis_send, dis_recv, ret_send, ret_recv, part_send, part_recv,
):
    ext = 128
    full = width + ext
    half = 4 * slots
    msg = 2 * half
    cover = 16 * half
    ctx, tp = lax.axis_index("ctx"), lax.axis_index("tp")
    c = ctx % 2
    me = (tp % 4, ctx // 8 * 2 + tp // 4, ctx // 2 % 4)
    mbit = tuple((v + c) % 2 for v in me)
    mine = mbit[2] * 4 + mbit[1] * 2 + mbit[0]
    my_expert = expert_of(me, c)

    def member(r):
        b = tuple(1 - v if t else v for v, t in zip(mbit, bits(r)))
        return b[2] * 4 + b[1] * 2 + b[0]

    def rows(start, size):
        return pl.ds(pl.multiple_of(start, 16), size)

    w_copies = [
        pltpu.make_async_copy(a, b, w_sem.at[i])
        for i, (a, b) in enumerate(((dw_hbm, dw), (gw_hbm, gw), (uw_hbm, uw)))
    ]
    for copy in w_copies:
        copy.start()

    s_copies = [
        pltpu.make_async_copy(a, b, w_sem.at[3 + i])
        for i, (a, b) in enumerate(((gate_hbm, sav_g), (up_hbm, sav_u)))
    ]
    for copy in s_copies:
        copy.start()

    def source_parts(sender, sc):
        out = []
        for v, part_of in zip(
            sender, (lambda x: x, lambda y: y // 2 * 64 + y % 2 * 4, lambda z: z * 16)
        ):
            low = v - (v + sc) % 2 + 4
            out.append((part_of(low % 4), part_of((low + 1) % 4)))
        return out

    def permute_saved(k):
        r = iota((msg, 1), 0)
        m = jnp.floor((r + 0.5) * (1.0 / slots))
        slot = r - m * slots
        mz = jnp.floor((m + 0.5) * 0.25)
        my = jnp.floor((m - 4 * mz + 0.5) * 0.5)
        mx = m - 4 * mz - 2 * my
        lanes = iota((1, cover * 2), 1)
        for q in range(4):
            p, sc = 2 * k + q // 2, q % 2
            parts = source_parts(flipped(me, FLIPS[p], sc, outer), sc)
            at = slot * (cover * 2 // slots) + 8.0 * sc
            for bit, (low, high) in zip((mx, my, mz), parts):
                at = at + jnp.where(bit > 0.5, high.astype(F32), low.astype(F32))
            perm[q * msg : (q + 1) * msg, :] = jnp.where(at == lanes, 1.0, 0.0).astype(BF)
        for src, dst in ((sav_g, gf), (sav_u, uf)):
            for n in range(hidden // 256):
                cols = slice(n * 256, (n + 1) * 256)
                dst[:, cols] = jnp.dot(perm[...], src[:, cols], preferred_element_type=F32).astype(BF)

    barrier = pltpu.get_barrier_semaphore()
    friends = [device(me, 1 - c)]
    for f in range(1, 8):
        friends.append(device(flipped(me, f, c, outer), c))
        friends.append(device(flipped(me, f, c, outer), 1 - c))
        friends.append(device(flipped(me, f, 1 - c, outer), 1 - c))
        friends.append(device(flipped(me, f, c, inner), c))
    for friend in friends:
        pl.semaphore_signal(barrier, inc=1, device_id=friend, device_id_type=MESH)

    own = rows(mine * tokens, tokens)
    tok[own, 0:width] = grad_ref[...]
    sub = lax.broadcasted_iota(jnp.int32, (ext, tokens), 0)
    sub64 = jnp.where(sub >= 64, sub - 64, sub)
    ids = ids_ref[...]
    combine = comb_ref[...].astype(F32)
    hot_t = jnp.zeros((ext, tokens), F32)
    weight_t = jnp.zeros((ext, tokens), F32)
    for k in range(ids.shape[0]):
        same = ids[k : k + 1, :] == sub64
        hot_t = jnp.where(same, 1.0, hot_t)
        weight_t = jnp.where(same, combine[k : k + 1, :], weight_t)
    row, col = iota((tokens, tokens), 0), iota((tokens, tokens), 1)
    lower = jnp.where(col < row, 1.0, 0.0).astype(BF)
    same = jnp.where(col == row, 1.0, 0.0).astype(BF)
    count = lax.dot_general(lower, hot_t.astype(BF), NT, preferred_element_type=F32)
    hot = lax.dot_general(same, hot_t.astype(BF), NT, preferred_element_type=F32)
    weight = lax.dot_general(same, weight_t.astype(BF), NT, preferred_element_type=F32)
    lane = lax.broadcasted_iota(jnp.int32, (tokens, ext), 1)
    table = jnp.where(lane < 64, jnp.where(hot > 0.5, count, -1.0), weight)
    tok[own, width:full] = table.astype(BF)

    with jax.named_scope("barrier"):
        pl.semaphore_wait(barrier, len(friends))

    def tok_copy(r):
        return pltpu.make_async_remote_copy(
            src_ref=tok.at[own],
            dst_ref=tok.at[own],
            send_sem=tok_send.at[r],
            recv_sem=tok_recv.at[r],
            device_id=device(flipped(me, r, c, inner), c),
            device_id_type=MESH,
        )

    def tok_arrival(r):
        there = rows(member(r) * tokens, tokens)
        return pltpu.make_async_remote_copy(
            src_ref=tok.at[there],
            dst_ref=tok.at[there],
            send_sem=tok_send.at[r],
            recv_sem=tok_recv.at[r],
            device_id=device(flipped(me, r, c, inner), c),
            device_id_type=MESH,
        )

    for r in range(1, 8):
        tok_copy(r).start()

    slane = lax.broadcasted_iota(jnp.int32, (half, ext), 1)
    for i in range(16):
        e = expert_of(flipped(me, FLIPS[i // 2], c, outer), i % 2)
        selp[i * half : (i + 1) * half, :] = jnp.where(slane == e, 1.0, 0.0).astype(BF)
        selw[i * half : (i + 1) * half, :] = jnp.where(slane == e + 64, 1.0, 0.0).astype(BF)

    def slot_of(j):
        block = jnp.floor((j + 0.5) * (1.0 / slots))
        group = jnp.floor((block + 0.5) * 0.25)
        return j - block * slots, block - group * 4

    def owner_of(t):
        return jnp.floor((t + 0.5) * (1.0 / tokens))

    def dis_copy(i, h, p, dc):
        here = rows(i * msg + h * half, half)
        there = rows((2 * p + c) * msg + h * half, half)
        dst = device(flipped(me, FLIPS[p], c, outer), dc)
        return pltpu.make_async_remote_copy(
            src_ref=stage.at[here, pl.ds(0, width)],
            dst_ref=recv.at[there],
            send_sem=dis_send.at[i * 2 + h],
            recv_sem=dis_recv.at[(2 * p + c) * 2 + h],
            device_id=dst,
            device_id_type=MESH,
        )

    def dis_self(h):
        here = rows(c * msg + h * half, half)
        return pltpu.make_async_copy(stage.at[here, pl.ds(0, width)], recv.at[here], l_sem.at[h])

    def dis_arrival(j, h):
        here = rows(j * msg + h * half, half)
        return pltpu.make_async_remote_copy(
            src_ref=stage.at[here, pl.ds(0, width)],
            dst_ref=recv.at[here],
            send_sem=dis_send.at[j * 2 + h],
            recv_sem=dis_recv.at[j * 2 + h],
            device_id=device(me, 1 - c),
            device_id_type=MESH,
        )

    for step in range(2):
        h = mbit[2] if step == 0 else 1 - mbit[2]
        with jax.named_scope("wait_tokens"):
            for r in range(4 * step, 4 * step + 4):
                if r > 0:
                    tok_arrival(r).wait_recv()
        there = rows(h * 4 * tokens, 4 * tokens)
        tables = tok[there, width:full]
        pos = lax.dot_general(selp[...], tables, NT, preferred_element_type=F32)
        slot, four = slot_of(iota((cover, 1), 0))
        owner = owner_of(iota((1, 4 * tokens), 1))
        sel[...] = jnp.where((pos == slot) & (four == owner), 1.0, 0.0).astype(BF)

        tile = 512

        @pl.loop(0, width // tile)
        def _(n):
            cols = pl.ds(pl.multiple_of(n * tile, tile), tile)
            got = jnp.dot(sel[...], tok[there, cols], preferred_element_type=F32).astype(BF)
            for i in range(16):
                stage[rows(i * msg + h * half, half), cols] = got[i * half : (i + 1) * half]

        dis_self(h).start()
        dis_copy(1 - c, h, 0, 1 - c).start()
        for p in range(1, 8):
            for dc in range(2):
                dis_copy(2 * p + dc, h, p, dc).start()

    slot, four = slot_of(iota((1, cover), 1))
    owner = owner_of(iota((4 * tokens, 1), 0))
    for h in range(2):
        tables = tok[h * 4 * tokens : (h + 1) * 4 * tokens, width:full]
        pos = lax.dot_general(tables, selp[...], NT, preferred_element_type=F32)
        wgt = lax.dot_general(tables, selw[...], NT, preferred_element_type=F32)
        hit = (pos == slot) & (four == owner)
        plac[h] = jnp.where(hit, 1.0, 0.0).astype(BF)
        wplac[h] = jnp.where(hit, wgt, 0.0).astype(BF)

    with jax.named_scope("wait_weights"):
        for copy in w_copies + s_copies:
            copy.wait()

    def ret_copy(j, h, p, dc):
        here = rows(j * msg + h * half, half)
        there = rows((2 * p + c) * half, half)
        return pltpu.make_async_remote_copy(
            src_ref=stage.at[here],
            dst_ref=ret.at[h, there],
            send_sem=ret_send.at[j * 2 + h],
            recv_sem=ret_recv.at[(2 * p + c) * 2 + h],
            device_id=device(flipped(me, FLIPS[p], dc, outer), dc),
            device_id_type=MESH,
        )

    def ret_self(h):
        here = rows(c * msg + h * half, half)
        return pltpu.make_async_copy(stage.at[here], ret.at[h, rows(c * half, half)], l_sem.at[2 + h])

    def ret_arrival(j, h):
        return pltpu.make_async_remote_copy(
            src_ref=stage.at[rows(j * msg + h * half, half)],
            dst_ref=ret.at[h, rows(j * half, half)],
            send_sem=ret_send.at[j * 2 + h],
            recv_sem=ret_recv.at[j * 2 + h],
            device_id=device(me, 1 - c),
            device_id_type=MESH,
        )

    batch = 4 * msg
    elane = lax.broadcasted_iota(jnp.int32, (batch, ext), 1)
    for k in range(4):
        with jax.named_scope("permute_saved"):
            permute_saved(k)
        with jax.named_scope("wait_rows"):
            for j in range(4 * k, 4 * k + 4):
                if j >= 2:
                    for h in range(2):
                        dis_arrival(j, h).wait_recv()
            if k == 0:
                for h in range(2):
                    dis_arrival(1 - c, h).wait_recv()
                    dis_self(h).wait()
        buf = gb.at[pl.ds((k % 2) * batch, batch)]
        load = pltpu.make_async_copy(recv.at[pl.ds(k * batch, batch)], buf, l_sem.at[4])
        with jax.named_scope("load_rows"):
            load.start()
            load.wait()

        cacc[...] = jnp.zeros_like(cacc)
        tile = 256

        @pl.loop(0, hidden // tile)
        def _(n):
            cols = pl.ds(pl.multiple_of(n * tile, tile), tile)
            dh = lax.dot_general(buf[...], dw[cols, :], NT, preferred_element_type=F32)
            g, u = gf[:, cols].astype(F32), uf[:, cols].astype(F32)
            sg = jax.nn.sigmoid(g)
            a = g * sg
            prod = a * u * dh
            total = cacc[...]
            for b in range(tile // ext):
                total = total + prod[:, b * ext : (b + 1) * ext]
            cacc[...] = total
            dg[:, cols] = (dh * u * sg * (1.0 + g * (1.0 - sg))).astype(BF)
            du[:, cols] = (dh * a).astype(BF)

        with jax.named_scope("wait_stage"):
            for j in range(4 * k, 4 * k + 4):
                if j >= 2:
                    for h in range(2):
                        dis_copy(j, h, j // 2, j % 2).wait_send()
            if k == 0:
                for h in range(2):
                    dis_copy(1 - c, h, 0, 1 - c).wait_send()

        here = pl.ds(k * batch, batch)
        comb = jnp.sum(cacc[...], axis=1, keepdims=True)
        stage[here, width:full] = jnp.where(elane == my_expert, comb, 0.0).astype(BF)
        xtile = 512

        @pl.loop(0, width // xtile)
        def _(n):
            cols = pl.ds(pl.multiple_of(n * xtile, xtile), xtile)
            x = lax.dot_general(dg[...], gw[cols, :], NT, preferred_element_type=F32)
            x = x + lax.dot_general(du[...], uw[cols, :], NT, preferred_element_type=F32)
            stage[here, cols] = x.astype(BF)

        if k == 0:
            for h in range(2):
                ret_self(h).start()
                ret_copy(1 - c, h, 0, 1 - c).start()
        for j in range(4 * k, 4 * k + 4):
            if j >= 2:
                for h in range(2):
                    ret_copy(j, h, j // 2, j % 2).start()

    for r in range(1, 8):
        tok_copy(r).wait_send()

    def part_copy(r):
        return pltpu.make_async_remote_copy(
            src_ref=tok.at[rows(member(r) * tokens, tokens)],
            dst_ref=part.at[pl.ds(r * tokens, tokens)],
            send_sem=part_send.at[r],
            recv_sem=part_recv.at[r],
            device_id=device(flipped(me, r, c, inner), c),
            device_id_type=MESH,
        )

    for step in range(2):
        h = 1 - mbit[2] if step == 0 else mbit[2]
        with jax.named_scope("wait_returns"):
            for j in range(2, 16):
                ret_arrival(j, h).wait_recv()
            ret_arrival(1 - c, h).wait_recv()
            ret_self(h).wait()
        loads = (
            pltpu.make_async_copy(ret.at[h, :, pl.ds(0, width)], gb, l_sem.at[5]),
            pltpu.make_async_copy(ret.at[h, :, pl.ds(width, ext)], rc, l_sem.at[6]),
        )
        with jax.named_scope("load_returns"):
            for load in loads:
                load.start()
            for load in loads:
                load.wait()
        there = rows(h * 4 * tokens, 4 * tokens)
        tok[there, width:full] = jnp.dot(plac[h], rc[...], preferred_element_type=F32).astype(BF)
        tile = 512

        @pl.loop(0, width // tile)
        def _(n):
            cols = pl.ds(pl.multiple_of(n * tile, tile), tile)
            tok[there, cols] = jnp.dot(wplac[h], gb[:, cols], preferred_element_type=F32).astype(BF)

        for r in range(4 - 4 * step, 8 - 4 * step):
            if r > 0:
                part_copy(r).start()

    with jax.named_scope("wait_parts"):
        for r in range(1, 8):
            part_copy(r).wait_recv()
    tile = 512

    @pl.loop(0, width // tile)
    def _(n):
        cols = pl.ds(pl.multiple_of(n * tile, tile), tile)
        total = tok[own, cols].astype(F32)
        for r in range(1, 8):
            total = total + part[r * tokens : (r + 1) * tokens, cols].astype(F32)
        out_ref[:, cols] = total.astype(BF)

    total = tok[own, width:full].astype(F32)
    for r in range(1, 8):
        total = total + part[r * tokens : (r + 1) * tokens, width:full].astype(F32)
    total = jnp.where(lane < 64, total, 0.0)
    same = jnp.where(iota((ext, ext), 0) == iota((ext, ext), 1), 1.0, 0.0).astype(BF)
    total_t = lax.dot_general(same, total.astype(BF), NT, preferred_element_type=F32)
    ksub = lax.broadcasted_iota(jnp.int32, ids.shape, 0)
    result = jnp.zeros(ids.shape, F32)
    for k in range(ids.shape[0]):
        value = jnp.sum(jnp.where(ids[k : k + 1, :] == sub, total_t, 0.0), axis=0, keepdims=True)
        result = jnp.where(ksub == k, value, result)
    outc_ref[...] = result.astype(BF)

    with jax.named_scope("wait_sends"):
        for r in range(1, 8):
            part_copy(r).wait_send()
        for h in range(2):
            ret_copy(1 - c, h, 0, 1 - c).wait_send()
            for j in range(2, 16):
                ret_copy(j, h, j // 2, j % 2).wait_send()


def body(grad_out, expert_ids, combine, gate_saved, up_saved, gate_weight, up_weight, down_weight):
    tokens, width = grad_out.shape
    sources, slots, hidden = gate_saved.shape
    top = expert_ids.shape[1]
    full = width + 128
    half = 4 * slots
    cover = 16 * half
    batch = 8 * half
    vmem = pl.BlockSpec(memory_space=pltpu.VMEM)
    hbm = pl.BlockSpec(memory_space=pl.ANY)
    dma = pltpu.SemaphoreType.DMA
    out = pl.pallas_call(
        functools.partial(kernel, tokens, slots, width, hidden),
        out_shape=(
            jax.ShapeDtypeStruct((tokens, width), BF),
            jax.ShapeDtypeStruct((top, tokens), BF),
            jax.ShapeDtypeStruct((2 * cover, width), BF),
            jax.ShapeDtypeStruct((2, cover, full), BF),
        ),
        in_specs=[vmem, vmem, vmem, hbm, hbm, hbm, hbm, hbm],
        out_specs=(vmem, vmem, hbm, hbm),
        scratch_shapes=[
            pltpu.VMEM((8 * tokens, full), BF),
            pltpu.VMEM((2 * cover, full), BF),
            pltpu.VMEM((width, hidden), BF),
            pltpu.VMEM((width, hidden), BF),
            pltpu.VMEM((hidden, width), BF),
            pltpu.VMEM((2 * cover, hidden), BF),
            pltpu.VMEM((2 * cover, hidden), BF),
            pltpu.VMEM((batch, hidden), BF),
            pltpu.VMEM((batch, hidden), BF),
            pltpu.VMEM((batch, hidden), BF),
            pltpu.VMEM((batch, hidden), BF),
            pltpu.VMEM((batch, 2 * cover), BF),
            pltpu.VMEM((batch, 128), F32),
            pltpu.VMEM((cover, width), BF),
            pltpu.VMEM((cover, 128), BF),
            pltpu.VMEM((cover, 4 * tokens), BF),
            pltpu.VMEM((cover, 128), BF),
            pltpu.VMEM((cover, 128), BF),
            pltpu.VMEM((2, 4 * tokens, cover), BF),
            pltpu.VMEM((2, 4 * tokens, cover), BF),
            pltpu.VMEM((8 * tokens, full), BF),
            dma((5,)),
            dma((7,)),
            dma((8,)),
            dma((8,)),
            dma((32,)),
            dma((32,)),
            dma((32,)),
            dma((32,)),
            dma((8,)),
            dma((8,)),
        ],
        compiler_params=pltpu.CompilerParams(
            collective_id=0, has_side_effects=True, vmem_limit_bytes=66 * 1000 * 1000
        ),
        cost_estimate=pl.CostEstimate(
            flops=6 * sources * slots * hidden * width,
            bytes_accessed=80_000_000,
            transcendentals=sources * slots * hidden,
        ),
    )(
        grad_out,
        expert_ids.T,
        combine.T,
        gate_saved.transpose(1, 0, 2).reshape(2 * cover, hidden),
        up_saved.transpose(1, 0, 2).reshape(2 * cover, hidden),
        gate_weight,
        up_weight,
        down_weight,
    )
    return out[0], out[1].T


def solution(mesh):
    placed = (
        P(("ctx", "tp"), None),
        P(("ctx", "tp"), None),
        P(("ctx", "tp"), None),
        P(None, None, ("ctx", "tp")),
        P(None, None, ("ctx", "tp")),
        P(None, ("ctx", "tp")),
        P(None, ("ctx", "tp")),
        P(("ctx", "tp"), None),
    )
    return jax.shard_map(
        body,
        mesh=mesh,
        in_specs=placed,
        out_specs=(P(("ctx", "tp"), None), P(("ctx", "tp"), None)),
        check_vma=False,
    )
```

```python
import functools

import jax
import jax.numpy as jnp
from jax import lax
from jax.experimental import pallas as pl
from jax.experimental.pallas import tpu as pltpu
from jax.sharding import PartitionSpec as P

MESH = pl.DeviceIdType.MESH
FLIPS = (0, 7, 1, 6, 2, 5, 3, 4)
BF = jnp.bfloat16
F32 = jnp.float32
NT = (((1,), (1,)), ((), ()))


def bits(f):
    return f & 1, (f >> 1) & 1, (f >> 2) & 1


def outer(v, c):
    return (v + 3 + 2 * ((v + c) % 2)) % 4


def inner(v, c):
    return (v + 1 + 2 * ((v + c) % 2)) % 4


def flipped(xyz, f, c, how):
    return tuple(how(v, c) if b else v for v, b in zip(xyz, bits(f)))


def device(xyz, c):
    x, y, z = xyz
    return ((y // 2 * 4 + z) * 2 + c, (y % 2) * 4 + x)


def expert_of(xyz, c):
    ctx, tp = device(xyz, c)
    return ctx * 4 + tp // 2


def iota(shape, dim):
    return lax.broadcasted_iota(jnp.int32, shape, dim).astype(F32)


def kernel(
    tokens, slots, width, hidden,
    grad_ref, ids_ref, comb_ref, gate_hbm, up_hbm, gw_hbm, uw_hbm, dw_hbm,
    out_ref, outc_ref, recv, ret,
    tok, stage, gw, uw, dw, sav_g, sav_u, gf, uf, dg, du, perm, cacc, gb, sel, selp, selw, plac, wplac, part,
    w_sem, l_sem, tok_send, tok_recv, dis_send, dis_recv, ret_send, ret_recv, part_send, part_recv,
):
    ext = 128
    full = width + ext
    half = 4 * slots
    msg = 2 * half
    cover = 16 * half
    ctx, tp = lax.axis_index("ctx"), lax.axis_index("tp")
    c = ctx % 2
    me = (tp % 4, ctx // 8 * 2 + tp // 4, ctx // 2 % 4)
    mbit = tuple((v + c) % 2 for v in me)
    mine = mbit[2] * 4 + mbit[1] * 2 + mbit[0]
    my_expert = expert_of(me, c)

    def member(r):
        b = tuple(1 - v if t else v for v, t in zip(mbit, bits(r)))
        return b[2] * 4 + b[1] * 2 + b[0]

    def rows(start, size):
        return pl.ds(pl.multiple_of(start, 16), size)

    w_copies = [
        pltpu.make_async_copy(a, b, w_sem.at[i])
        for i, (a, b) in enumerate(((dw_hbm, dw), (gw_hbm, gw), (uw_hbm, uw)))
    ]
    for copy in w_copies:
        copy.start()

    s_copies = [
        pltpu.make_async_copy(a, b, w_sem.at[3 + i])
        for i, (a, b) in enumerate(((gate_hbm, sav_g), (up_hbm, sav_u)))
    ]
    for copy in s_copies:
        copy.start()

    def source_parts(sender, sc):
        out = []
        for v, part_of in zip(
            sender, (lambda x: x, lambda y: y // 2 * 64 + y % 2 * 4, lambda z: z * 16)
        ):
            low = v - (v + sc) % 2 + 4
            out.append((part_of(low % 4), part_of((low + 1) % 4)))
        return out

    def permute_saved(k):
        r = iota((msg, 1), 0)
        m = jnp.floor((r + 0.5) * (1.0 / slots))
        slot = r - m * slots
        mz = jnp.floor((m + 0.5) * 0.25)
        my = jnp.floor((m - 4 * mz + 0.5) * 0.5)
        mx = m - 4 * mz - 2 * my
        lanes = iota((1, cover * 2), 1)
        for q in range(4):
            p, sc = 2 * k + q // 2, q % 2
            parts = source_parts(flipped(me, FLIPS[p], sc, outer), sc)
            at = slot * (cover * 2 // slots) + 8.0 * sc
            for bit, (low, high) in zip((mx, my, mz), parts):
                at = at + jnp.where(bit > 0.5, high.astype(F32), low.astype(F32))
            perm[q * msg : (q + 1) * msg, :] = jnp.where(at == lanes, 1.0, 0.0).astype(BF)
        for src, dst in ((sav_g, gf), (sav_u, uf)):
            for n in range(hidden // 256):
                cols = slice(n * 256, (n + 1) * 256)
                dst[:, cols] = jnp.dot(perm[...], src[:, cols], preferred_element_type=F32).astype(BF)

    barrier = pltpu.get_barrier_semaphore()
    friends = [device(me, 1 - c)]
    for f in range(1, 8):
        friends.append(device(flipped(me, f, c, outer), c))
        friends.append(device(flipped(me, f, c, outer), 1 - c))
        friends.append(device(flipped(me, f, 1 - c, outer), 1 - c))
        friends.append(device(flipped(me, f, c, inner), c))
    for friend in friends:
        pl.semaphore_signal(barrier, inc=1, device_id=friend, device_id_type=MESH)

    own = rows(mine * tokens, tokens)
    tok[own, 0:width] = grad_ref[...]
    sub = lax.broadcasted_iota(jnp.int32, (ext, tokens), 0)
    sub64 = jnp.where(sub >= 64, sub - 64, sub)
    ids = ids_ref[...]
    combine = comb_ref[...].astype(F32)
    hot_t = jnp.zeros((ext, tokens), F32)
    weight_t = jnp.zeros((ext, tokens), F32)
    for k in range(ids.shape[0]):
        same = ids[k : k + 1, :] == sub64
        hot_t = jnp.where(same, 1.0, hot_t)
        weight_t = jnp.where(same, combine[k : k + 1, :], weight_t)
    row, col = iota((tokens, tokens), 0), iota((tokens, tokens), 1)
    lower = jnp.where(col < row, 1.0, 0.0).astype(BF)
    same = jnp.where(col == row, 1.0, 0.0).astype(BF)
    count = lax.dot_general(lower, hot_t.astype(BF), NT, preferred_element_type=F32)
    hot = lax.dot_general(same, hot_t.astype(BF), NT, preferred_element_type=F32)
    weight = lax.dot_general(same, weight_t.astype(BF), NT, preferred_element_type=F32)
    lane = lax.broadcasted_iota(jnp.int32, (tokens, ext), 1)
    table = jnp.where(lane < 64, jnp.where(hot > 0.5, count, -1.0), weight)
    tok[own, width:full] = table.astype(BF)

    with jax.named_scope("barrier"):
        pl.semaphore_wait(barrier, len(friends))

    third = full // 3
    parts = [pl.ds(a * third, third) for a in range(3)]
    def relative(a, r):
        return sum(((r >> i) & 1) << ((a + i) % 3) for i in range(3))

    def partner(a, stage_):
        return device(flipped(me, 1 << ((a + stage_) % 3), c, inner), c)

    def tok_copy(a, r, stage_):
        block = tok.at[rows(member(relative(a, r)) * tokens, tokens), parts[a]]
        return pltpu.make_async_remote_copy(
            src_ref=block,
            dst_ref=block,
            send_sem=tok_send.at[a * 8 + r + (1 << stage_)],
            recv_sem=tok_recv.at[a * 8 + r + (1 << stage_)],
            device_id=partner(a, stage_),
            device_id_type=MESH,
        )

    def tok_arrival(a, r):
        stage_ = r.bit_length() - 1
        block = tok.at[rows(member(relative(a, r)) * tokens, tokens), parts[a]]
        return pltpu.make_async_remote_copy(
            src_ref=block,
            dst_ref=block,
            send_sem=tok_send.at[a * 8 + r],
            recv_sem=tok_recv.at[a * 8 + r],
            device_id=partner(a, stage_),
            device_id_type=MESH,
        )

    for stage_ in range(3):
        for a in range(3):
            tok_copy(a, 0, stage_).start()

    slane = lax.broadcasted_iota(jnp.int32, (half, ext), 1)
    for i in range(16):
        e = expert_of(flipped(me, FLIPS[i // 2], c, outer), i % 2)
        selp[i * half : (i + 1) * half, :] = jnp.where(slane == e, 1.0, 0.0).astype(BF)
        selw[i * half : (i + 1) * half, :] = jnp.where(slane == e + 64, 1.0, 0.0).astype(BF)

    def slot_of(j):
        block = jnp.floor((j + 0.5) * (1.0 / slots))
        group = jnp.floor((block + 0.5) * 0.25)
        return j - block * slots, block - group * 4

    def owner_of(t):
        return jnp.floor((t + 0.5) * (1.0 / tokens))

    def dis_copy(i, h, p, dc):
        here = rows(i * msg + h * half, half)
        there = rows((2 * p + c) * msg + h * half, half)
        dst = device(flipped(me, FLIPS[p], c, outer), dc)
        return pltpu.make_async_remote_copy(
            src_ref=stage.at[here, pl.ds(0, width)],
            dst_ref=recv.at[there],
            send_sem=dis_send.at[i * 2 + h],
            recv_sem=dis_recv.at[(2 * p + c) * 2 + h],
            device_id=dst,
            device_id_type=MESH,
        )

    def dis_self(h):
        here = rows(c * msg + h * half, half)
        return pltpu.make_async_copy(stage.at[here, pl.ds(0, width)], recv.at[here], l_sem.at[h])

    def dis_arrival(j, h):
        here = rows(j * msg + h * half, half)
        return pltpu.make_async_remote_copy(
            src_ref=stage.at[here, pl.ds(0, width)],
            dst_ref=recv.at[here],
            send_sem=dis_send.at[j * 2 + h],
            recv_sem=dis_recv.at[j * 2 + h],
            device_id=device(me, 1 - c),
            device_id_type=MESH,
        )

    with jax.named_scope("forward_tokens"):
        for r in range(1, 4):
            for a in range(3):
                tok_arrival(a, r).wait_recv()
                for stage_ in range(r.bit_length(), 3):
                    tok_copy(a, r, stage_).start()

    for step in range(2):
        h = mbit[2] if step == 0 else 1 - mbit[2]
        with jax.named_scope("wait_tokens"):
            for r in range(4, 8):
                for a in range(3):
                    if (relative(a, r) >> 2) == step:
                        tok_arrival(a, r).wait_recv()
        there = rows(h * 4 * tokens, 4 * tokens)
        tables = tok[there, width:full]
        pos = lax.dot_general(selp[...], tables, NT, preferred_element_type=F32)
        slot, four = slot_of(iota((cover, 1), 0))
        owner = owner_of(iota((1, 4 * tokens), 1))
        sel[...] = jnp.where((pos == slot) & (four == owner), 1.0, 0.0).astype(BF)

        tile = 512

        @pl.loop(0, width // tile)
        def _(n):
            cols = pl.ds(pl.multiple_of(n * tile, tile), tile)
            got = jnp.dot(sel[...], tok[there, cols], preferred_element_type=F32).astype(BF)
            for i in range(16):
                stage[rows(i * msg + h * half, half), cols] = got[i * half : (i + 1) * half]

        dis_self(h).start()
        dis_copy(1 - c, h, 0, 1 - c).start()
        for p in range(1, 8):
            for dc in range(2):
                dis_copy(2 * p + dc, h, p, dc).start()

    slot, four = slot_of(iota((1, cover), 1))
    owner = owner_of(iota((4 * tokens, 1), 0))
    for h in range(2):
        tables = tok[h * 4 * tokens : (h + 1) * 4 * tokens, width:full]
        pos = lax.dot_general(tables, selp[...], NT, preferred_element_type=F32)
        wgt = lax.dot_general(tables, selw[...], NT, preferred_element_type=F32)
        hit = (pos == slot) & (four == owner)
        plac[h] = jnp.where(hit, 1.0, 0.0).astype(BF)
        wplac[h] = jnp.where(hit, wgt, 0.0).astype(BF)

    with jax.named_scope("wait_weights"):
        for copy in w_copies + s_copies:
            copy.wait()

    def ret_at(j, h, a):
        return j * 2 + h if a is None else 32 + ((j - 12) * 2 + h) * 3 + a

    def ret_cols(a):
        return pl.ds(0, full) if a is None else parts[a]

    def ret_copy(j, h, p, dc, a=None):
        here = rows(j * msg + h * half, half)
        there = rows((2 * p + c) * half, half)
        return pltpu.make_async_remote_copy(
            src_ref=stage.at[here, ret_cols(a)],
            dst_ref=ret.at[h, there, ret_cols(a)],
            send_sem=ret_send.at[ret_at(j, h, a)],
            recv_sem=ret_recv.at[ret_at(2 * p + c, h, a)],
            device_id=device(flipped(me, FLIPS[p], dc, outer), dc),
            device_id_type=MESH,
        )

    def ret_self(h):
        here = rows(c * msg + h * half, half)
        return pltpu.make_async_copy(stage.at[here], ret.at[h, rows(c * half, half)], l_sem.at[2 + h])

    def ret_arrival(j, h, a=None):
        return pltpu.make_async_remote_copy(
            src_ref=stage.at[rows(j * msg + h * half, half), ret_cols(a)],
            dst_ref=ret.at[h, rows(j * half, half), ret_cols(a)],
            send_sem=ret_send.at[ret_at(j, h, a)],
            recv_sem=ret_recv.at[ret_at(j, h, a)],
            device_id=device(me, 1 - c),
            device_id_type=MESH,
        )

    batch = 4 * msg
    elane = lax.broadcasted_iota(jnp.int32, (batch, ext), 1)
    for k in range(4):
        with jax.named_scope("permute_saved"):
            permute_saved(k)
        with jax.named_scope("wait_rows"):
            for j in range(4 * k, 4 * k + 4):
                if j >= 2:
                    for h in range(2):
                        dis_arrival(j, h).wait_recv()
            if k == 0:
                for h in range(2):
                    dis_arrival(1 - c, h).wait_recv()
                    dis_self(h).wait()
        buf = gb.at[pl.ds((k % 2) * batch, batch)]
        load = pltpu.make_async_copy(recv.at[pl.ds(k * batch, batch)], buf, l_sem.at[4])
        with jax.named_scope("load_rows"):
            load.start()
            load.wait()

        cacc[...] = jnp.zeros_like(cacc)
        tile = 256

        @pl.loop(0, hidden // tile)
        def _(n):
            cols = pl.ds(pl.multiple_of(n * tile, tile), tile)
            dh = lax.dot_general(buf[...], dw[cols, :], NT, preferred_element_type=F32)
            g, u = gf[:, cols].astype(F32), uf[:, cols].astype(F32)
            sg = jax.nn.sigmoid(g)
            a = g * sg
            prod = a * u * dh
            total = cacc[...]
            for b in range(tile // ext):
                total = total + prod[:, b * ext : (b + 1) * ext]
            cacc[...] = total
            dg[:, cols] = (dh * u * sg * (1.0 + g * (1.0 - sg))).astype(BF)
            du[:, cols] = (dh * a).astype(BF)

        with jax.named_scope("wait_stage"):
            for j in range(4 * k, 4 * k + 4):
                if j >= 2:
                    for h in range(2):
                        dis_copy(j, h, j // 2, j % 2).wait_send()
            if k == 0:
                for h in range(2):
                    dis_copy(1 - c, h, 0, 1 - c).wait_send()

        here = pl.ds(k * batch, batch)
        comb = jnp.sum(cacc[...], axis=1, keepdims=True)
        stage[here, width:full] = jnp.where(elane == my_expert, comb, 0.0).astype(BF)
        for a in range(3):
            cols = pl.ds(a * third, min(third, width - a * third))
            x = lax.dot_general(dg[...], gw[cols, :], NT, preferred_element_type=F32)
            x = x + lax.dot_general(du[...], uw[cols, :], NT, preferred_element_type=F32)
            stage[here, cols] = x.astype(BF)
            if k == 3:
                for j in range(12, 16):
                    for h in range(2):
                        ret_copy(j, h, j // 2, j % 2, a).start()
        if k == 0:
            for h in range(2):
                ret_self(h).start()
                ret_copy(1 - c, h, 0, 1 - c).start()
        if k < 3:
            for j in range(max(4 * k, 2), 4 * k + 4):
                for h in range(2):
                    ret_copy(j, h, j // 2, j % 2).start()

    for a in range(3):
        for r in range(1, 8):
            tok_arrival(a, r).wait_send()

    def part_copy(a, r):
        stage_ = r.bit_length() - 1
        return pltpu.make_async_remote_copy(
            src_ref=tok.at[rows(member(relative(a, r)) * tokens, tokens), parts[a]],
            dst_ref=part.at[pl.ds(r * tokens, tokens), parts[a]],
            send_sem=part_send.at[a * 8 + r],
            recv_sem=part_recv.at[a * 8 + r],
            device_id=partner(a, stage_),
            device_id_type=MESH,
        )

    def combine_part(a):
        loads = []
        for h in range(2):
            loads.append(
                pltpu.make_async_copy(
                    ret.at[h, :, parts[a]], gb.at[:, pl.ds(h * third, third)], l_sem.at[5 + h]
                )
            )
        with jax.named_scope("load_returns"):
            for load in loads:
                load.start()
        for h, load in enumerate(loads):
            load.wait()
            there = pl.ds(h * 4 * tokens, 4 * tokens)
            size = min(third, width - a * third)
            got = gb[:, h * third : h * third + size]
            tok[there, a * third : a * third + size] = jnp.dot(
                wplac[h], got, preferred_element_type=F32
            ).astype(BF)
            if size < third:
                got = gb[:, h * third + size : (h + 1) * third]
                tok[there, width:full] = jnp.dot(plac[h], got, preferred_element_type=F32).astype(BF)
        for r in range(4, 8):
            part_copy(a, r).start()

    def gathered(a, r, first):
        cols = slice(a * third, (a + 1) * third)
        total = tok[rows(member(relative(a, r)) * tokens, tokens), cols].astype(F32)
        for stage_ in range(2, first - 1, -1):
            at = r + (1 << stage_)
            total = total + part[at * tokens : (at + 1) * tokens, cols].astype(F32)
        return total

    def pass_on(a, stage_):
        with jax.named_scope("wait_parts"):
            for r in range(1 << stage_, 2 << stage_):
                part_copy(a, r).wait_recv()
        if stage_ == 0:
            return
        for r in range(1 << (stage_ - 1), 1 << stage_):
            cols = slice(a * third, (a + 1) * third)
            tok[rows(member(relative(a, r)) * tokens, tokens), cols] = gathered(a, r, stage_).astype(BF)
            part_copy(a, r).start()

    with jax.named_scope("wait_returns"):
        for h in range(2):
            for j in range(2, 12):
                ret_arrival(j, h).wait_recv()
            ret_arrival(1 - c, h).wait_recv()
            ret_self(h).wait()

    def wait_last(a):
        with jax.named_scope("wait_last"):
            for h in range(2):
                for j in range(12, 16):
                    ret_arrival(j, h, a).wait_recv()

    wait_last(0)
    combine_part(0)
    wait_last(1)
    combine_part(1)
    pass_on(0, 2)
    wait_last(2)
    combine_part(2)
    pass_on(1, 2)
    pass_on(0, 1)
    pass_on(2, 2)
    pass_on(1, 1)
    pass_on(2, 1)
    for a in range(3):
        pass_on(a, 0)
        total = gathered(a, 0, 0)
        if a < 2:
            out_ref[:, a * third : (a + 1) * third] = total.astype(BF)
        else:
            out_ref[:, 2 * third : width] = total[:, : width - 2 * third].astype(BF)
            total = total[:, width - 2 * third :]
    total = jnp.where(lane < 64, total, 0.0)
    same = jnp.where(iota((ext, ext), 0) == iota((ext, ext), 1), 1.0, 0.0).astype(BF)
    total_t = lax.dot_general(same, total.astype(BF), NT, preferred_element_type=F32)
    ksub = lax.broadcasted_iota(jnp.int32, ids.shape, 0)
    result = jnp.zeros(ids.shape, F32)
    for k in range(ids.shape[0]):
        value = jnp.sum(jnp.where(ids[k : k + 1, :] == sub, total_t, 0.0), axis=0, keepdims=True)
        result = jnp.where(ksub == k, value, result)
    outc_ref[...] = result.astype(BF)

    with jax.named_scope("wait_sends"):
        for a in range(3):
            for r in range(1, 8):
                part_copy(a, r).wait_send()
        for h in range(2):
            ret_copy(1 - c, h, 0, 1 - c).wait_send()
            for j in range(2, 12):
                ret_copy(j, h, j // 2, j % 2).wait_send()
            for j in range(12, 16):
                for a in range(3):
                    ret_copy(j, h, j // 2, j % 2, a).wait_send()


def body(grad_out, expert_ids, combine, gate_saved, up_saved, gate_weight, up_weight, down_weight):
    tokens, width = grad_out.shape
    sources, slots, hidden = gate_saved.shape
    top = expert_ids.shape[1]
    full = width + 128
    half = 4 * slots
    cover = 16 * half
    batch = 8 * half
    vmem = pl.BlockSpec(memory_space=pltpu.VMEM)
    hbm = pl.BlockSpec(memory_space=pl.ANY)
    dma = pltpu.SemaphoreType.DMA
    out = pl.pallas_call(
        functools.partial(kernel, tokens, slots, width, hidden),
        out_shape=(
            jax.ShapeDtypeStruct((tokens, width), BF),
            jax.ShapeDtypeStruct((top, tokens), BF),
            jax.ShapeDtypeStruct((2 * cover, width), BF),
            jax.ShapeDtypeStruct((2, cover, full), BF),
        ),
        in_specs=[vmem, vmem, vmem, hbm, hbm, hbm, hbm, hbm],
        out_specs=(vmem, vmem, hbm, hbm),
        scratch_shapes=[
            pltpu.VMEM((8 * tokens, full), BF),
            pltpu.VMEM((2 * cover, full), BF),
            pltpu.VMEM((width, hidden), BF),
            pltpu.VMEM((width, hidden), BF),
            pltpu.VMEM((hidden, width), BF),
            pltpu.VMEM((2 * cover, hidden), BF),
            pltpu.VMEM((2 * cover, hidden), BF),
            pltpu.VMEM((batch, hidden), BF),
            pltpu.VMEM((batch, hidden), BF),
            pltpu.VMEM((batch, hidden), BF),
            pltpu.VMEM((batch, hidden), BF),
            pltpu.VMEM((batch, 2 * cover), BF),
            pltpu.VMEM((batch, 128), F32),
            pltpu.VMEM((cover, width), BF),
            pltpu.VMEM((cover, 4 * tokens), BF),
            pltpu.VMEM((cover, 128), BF),
            pltpu.VMEM((cover, 128), BF),
            pltpu.VMEM((2, 4 * tokens, cover), BF),
            pltpu.VMEM((2, 4 * tokens, cover), BF),
            pltpu.VMEM((8 * tokens, full), BF),
            dma((5,)),
            dma((7,)),
            dma((24,)),
            dma((24,)),
            dma((32,)),
            dma((32,)),
            dma((56,)),
            dma((56,)),
            dma((24,)),
            dma((24,)),
        ],
        compiler_params=pltpu.CompilerParams(
            collective_id=0, has_side_effects=True, vmem_limit_bytes=66 * 1000 * 1000
        ),
        cost_estimate=pl.CostEstimate(
            flops=6 * sources * slots * hidden * width,
            bytes_accessed=80_000_000,
            transcendentals=sources * slots * hidden,
        ),
    )(
        grad_out,
        expert_ids.T,
        combine.T,
        gate_saved.transpose(1, 0, 2).reshape(2 * cover, hidden),
        up_saved.transpose(1, 0, 2).reshape(2 * cover, hidden),
        gate_weight,
        up_weight,
        down_weight,
    )
    return out[0], out[1].T


def solution(mesh):
    placed = (
        P(("ctx", "tp"), None),
        P(("ctx", "tp"), None),
        P(("ctx", "tp"), None),
        P(None, None, ("ctx", "tp")),
        P(None, None, ("ctx", "tp")),
        P(None, ("ctx", "tp")),
        P(None, ("ctx", "tp")),
        P(("ctx", "tp"), None),
    )
    return jax.shard_map(
        body,
        mesh=mesh,
        in_specs=placed,
        out_specs=(P(("ctx", "tp"), None), P(("ctx", "tp"), None)),
        check_vma=False,
    )
```

```python
import functools

import jax
import jax.numpy as jnp
from jax import lax
from jax.experimental import pallas as pl
from jax.experimental.pallas import tpu as pltpu
from jax.sharding import PartitionSpec as P

MESH = pl.DeviceIdType.MESH
FLIPS = (0, 7, 1, 6, 2, 5, 3, 4)
BF = jnp.bfloat16
F32 = jnp.float32
NT = (((1,), (1,)), ((), ()))


def bits(f):
    return f & 1, (f >> 1) & 1, (f >> 2) & 1


def outer(v, c):
    return (v + 3 + 2 * ((v + c) % 2)) % 4


def inner(v, c):
    return (v + 1 + 2 * ((v + c) % 2)) % 4


def flipped(xyz, f, c, how):
    return tuple(how(v, c) if b else v for v, b in zip(xyz, bits(f)))


def device(xyz, c):
    x, y, z = xyz
    return ((y // 2 * 4 + z) * 2 + c, (y % 2) * 4 + x)


def expert_of(xyz, c):
    ctx, tp = device(xyz, c)
    return ctx * 4 + tp // 2


def iota(shape, dim):
    return lax.broadcasted_iota(jnp.int32, shape, dim).astype(F32)


def kernel(
    tokens, slots, width, hidden,
    grad_ref, ids_ref, comb_ref, gate_hbm, up_hbm, gw_hbm, uw_hbm, dw_hbm,
    out_ref, outc_ref, recv, ret,
    tok, stage, gw, uw, dw, sav_g, sav_u, gf, uf, dg, du, perm, cacc, gb, sel, selp, selw, plac, wplac, part,
    w_sem, l_sem, tok_send, tok_recv, dis_send, dis_recv, ret_send, ret_recv, part_send, part_recv,
):
    ext = 128
    full = width + ext
    half = 4 * slots
    msg = 2 * half
    cover = 16 * half
    ctx, tp = lax.axis_index("ctx"), lax.axis_index("tp")
    c = ctx % 2
    me = (tp % 4, ctx // 8 * 2 + tp // 4, ctx // 2 % 4)
    mbit = tuple((v + c) % 2 for v in me)
    mine = mbit[2] * 4 + mbit[1] * 2 + mbit[0]
    my_expert = expert_of(me, c)

    def member(r):
        b = tuple(1 - v if t else v for v, t in zip(mbit, bits(r)))
        return b[2] * 4 + b[1] * 2 + b[0]

    def rows(start, size):
        return pl.ds(pl.multiple_of(start, 16), size)

    w_copies = [
        pltpu.make_async_copy(a, b, w_sem.at[i])
        for i, (a, b) in enumerate(((dw_hbm, dw), (gw_hbm, gw), (uw_hbm, uw)))
    ]
    for copy in w_copies:
        copy.start()

    s_copies = [
        pltpu.make_async_copy(a, b, w_sem.at[3 + i])
        for i, (a, b) in enumerate(((gate_hbm, sav_g), (up_hbm, sav_u)))
    ]
    for copy in s_copies:
        copy.start()

    def source_parts(sender, sc):
        out = []
        for v, part_of in zip(
            sender, (lambda x: x, lambda y: y // 2 * 64 + y % 2 * 4, lambda z: z * 16)
        ):
            low = v - (v + sc) % 2 + 4
            out.append((part_of(low % 4), part_of((low + 1) % 4)))
        return out

    def permute_saved(k):
        r = iota((msg, 1), 0)
        m = jnp.floor((r + 0.5) * (1.0 / slots))
        slot = r - m * slots
        mz = jnp.floor((m + 0.5) * 0.25)
        my = jnp.floor((m - 4 * mz + 0.5) * 0.5)
        mx = m - 4 * mz - 2 * my
        lanes = iota((1, cover * 2), 1)
        for q in range(4):
            p, sc = 2 * k + q // 2, q % 2
            parts = source_parts(flipped(me, FLIPS[p], sc, outer), sc)
            at = slot * (cover * 2 // slots) + 8.0 * sc
            for bit, (low, high) in zip((mx, my, mz), parts):
                at = at + jnp.where(bit > 0.5, high.astype(F32), low.astype(F32))
            perm[q * msg : (q + 1) * msg, :] = jnp.where(at == lanes, 1.0, 0.0).astype(BF)
        for src, dst in ((sav_g, gf), (sav_u, uf)):
            for n in range(hidden // 256):
                cols = slice(n * 256, (n + 1) * 256)
                dst[:, cols] = jnp.dot(perm[...], src[:, cols], preferred_element_type=F32).astype(BF)

    barrier = pltpu.get_barrier_semaphore()
    friends = [device(me, 1 - c)]
    for f in range(1, 8):
        friends.append(device(flipped(me, f, c, outer), c))
        friends.append(device(flipped(me, f, c, outer), 1 - c))
        friends.append(device(flipped(me, f, 1 - c, outer), 1 - c))
        friends.append(device(flipped(me, f, c, inner), c))
    for friend in friends:
        pl.semaphore_signal(barrier, inc=1, device_id=friend, device_id_type=MESH)

    own = rows(mine * tokens, tokens)
    tok[own, 0:width] = grad_ref[...]
    sub = lax.broadcasted_iota(jnp.int32, (ext, tokens), 0)
    sub64 = jnp.where(sub >= 64, sub - 64, sub)
    ids = ids_ref[...]
    combine = comb_ref[...].astype(F32)
    hot_t = jnp.zeros((ext, tokens), F32)
    weight_t = jnp.zeros((ext, tokens), F32)
    for k in range(ids.shape[0]):
        same = ids[k : k + 1, :] == sub64
        hot_t = jnp.where(same, 1.0, hot_t)
        weight_t = jnp.where(same, combine[k : k + 1, :], weight_t)
    row, col = iota((tokens, tokens), 0), iota((tokens, tokens), 1)
    lower = jnp.where(col < row, 1.0, 0.0).astype(BF)
    same = jnp.where(col == row, 1.0, 0.0).astype(BF)
    count = lax.dot_general(lower, hot_t.astype(BF), NT, preferred_element_type=F32)
    hot = lax.dot_general(same, hot_t.astype(BF), NT, preferred_element_type=F32)
    weight = lax.dot_general(same, weight_t.astype(BF), NT, preferred_element_type=F32)
    lane = lax.broadcasted_iota(jnp.int32, (tokens, ext), 1)
    table = jnp.where(lane < 64, jnp.where(hot > 0.5, count, -1.0), weight)
    tok[own, width:full] = table.astype(BF)

    with jax.named_scope("barrier"):
        pl.semaphore_wait(barrier, len(friends))

    third = full // 3
    parts = [pl.ds(a * third, third) for a in range(3)]
    piece = 6 * ext
    sums = [pl.ds(a * piece, min(piece, full - a * piece)) for a in range(-(-full // piece))]

    def relative(a, r):
        return sum(((r >> i) & 1) << ((a + i) % 3) for i in range(3))

    def partner(a, stage_):
        return device(flipped(me, 1 << ((a + stage_) % 3), c, inner), c)

    def tok_copy(a, r, stage_):
        block = tok.at[rows(member(relative(a, r)) * tokens, tokens), parts[a]]
        return pltpu.make_async_remote_copy(
            src_ref=block,
            dst_ref=block,
            send_sem=tok_send.at[a * 8 + r + (1 << stage_)],
            recv_sem=tok_recv.at[a * 8 + r + (1 << stage_)],
            device_id=partner(a, stage_),
            device_id_type=MESH,
        )

    def tok_arrival(a, r):
        stage_ = r.bit_length() - 1
        block = tok.at[rows(member(relative(a, r)) * tokens, tokens), parts[a]]
        return pltpu.make_async_remote_copy(
            src_ref=block,
            dst_ref=block,
            send_sem=tok_send.at[a * 8 + r],
            recv_sem=tok_recv.at[a * 8 + r],
            device_id=partner(a, stage_),
            device_id_type=MESH,
        )

    for stage_ in range(3):
        for a in range(3):
            tok_copy(a, 0, stage_).start()

    slane = lax.broadcasted_iota(jnp.int32, (half, ext), 1)
    for i in range(16):
        e = expert_of(flipped(me, FLIPS[i // 2], c, outer), i % 2)
        selp[i * half : (i + 1) * half, :] = jnp.where(slane == e, 1.0, 0.0).astype(BF)
        selw[i * half : (i + 1) * half, :] = jnp.where(slane == e + 64, 1.0, 0.0).astype(BF)

    def slot_of(j):
        block = jnp.floor((j + 0.5) * (1.0 / slots))
        group = jnp.floor((block + 0.5) * 0.25)
        return j - block * slots, block - group * 4

    def owner_of(t):
        return jnp.floor((t + 0.5) * (1.0 / tokens))

    def dis_copy(i, h, p, dc):
        here = rows(i * msg + h * half, half)
        there = rows((2 * p + c) * msg + h * half, half)
        dst = device(flipped(me, FLIPS[p], c, outer), dc)
        return pltpu.make_async_remote_copy(
            src_ref=stage.at[here, pl.ds(0, width)],
            dst_ref=recv.at[there],
            send_sem=dis_send.at[i * 2 + h],
            recv_sem=dis_recv.at[(2 * p + c) * 2 + h],
            device_id=dst,
            device_id_type=MESH,
        )

    def dis_self(h):
        here = rows(c * msg + h * half, half)
        return pltpu.make_async_copy(stage.at[here, pl.ds(0, width)], recv.at[here], l_sem.at[h])

    def dis_arrival(j, h):
        here = rows(j * msg + h * half, half)
        return pltpu.make_async_remote_copy(
            src_ref=stage.at[here, pl.ds(0, width)],
            dst_ref=recv.at[here],
            send_sem=dis_send.at[j * 2 + h],
            recv_sem=dis_recv.at[j * 2 + h],
            device_id=device(me, 1 - c),
            device_id_type=MESH,
        )

    def dis_start(h, k):
        if k == 0:
            dis_self(h).start()
            dis_copy(1 - c, h, 0, 1 - c).start()
        for j in range(max(4 * k, 2), 4 * k + 4):
            dis_copy(j, h, j // 2, j % 2).start()

    def dis_sent(k):
        if k == 0:
            for h in range(2):
                dis_copy(1 - c, h, 0, 1 - c).wait_send()
        for j in range(max(4 * k, 2), 4 * k + 4):
            for h in range(2):
                dis_copy(j, h, j // 2, j % 2).wait_send()

    def select(step, h, later):
        there = rows(h * 4 * tokens, 4 * tokens)
        size = cover // 2
        tile = 512

        @pl.loop(0, width // tile)
        def _(n):
            cols = pl.ds(pl.multiple_of(n * tile, tile), tile)
            chosen = sel[step, later * size : (later + 1) * size]
            got = jnp.dot(chosen, tok[there, cols], preferred_element_type=F32).astype(BF)
            for i in range(8):
                stage[rows((8 * later + i) * msg + h * half, half), cols] = got[i * half : (i + 1) * half]

    with jax.named_scope("forward_tokens"):
        for r in range(1, 4):
            for a in range(3):
                tok_arrival(a, r).wait_recv()
                for stage_ in range(r.bit_length(), 3):
                    tok_copy(a, r, stage_).start()

    for step in range(2):
        h = mbit[2] if step == 0 else 1 - mbit[2]
        with jax.named_scope("wait_tokens"):
            for r in range(4, 8):
                for a in range(3):
                    if (relative(a, r) >> 2) == step:
                        tok_arrival(a, r).wait_recv()
        there = rows(h * 4 * tokens, 4 * tokens)
        tables = tok[there, width:full]
        pos = lax.dot_general(selp[...], tables, NT, preferred_element_type=F32)
        slot, four = slot_of(iota((cover, 1), 0))
        owner = owner_of(iota((1, 4 * tokens), 1))
        sel[step] = jnp.where((pos == slot) & (four == owner), 1.0, 0.0).astype(BF)

        select(step, h, 0)
        dis_start(h, 0)
        dis_start(h, 1)

    for step in range(2):
        select(step, mbit[2] if step == 0 else 1 - mbit[2], 1)

    slot, four = slot_of(iota((1, cover), 1))
    owner = owner_of(iota((4 * tokens, 1), 0))
    for h in range(2):
        tables = tok[h * 4 * tokens : (h + 1) * 4 * tokens, width:full]
        pos = lax.dot_general(tables, selp[...], NT, preferred_element_type=F32)
        wgt = lax.dot_general(tables, selw[...], NT, preferred_element_type=F32)
        hit = (pos == slot) & (four == owner)
        plac[h] = jnp.where(hit, 1.0, 0.0).astype(BF)
        wplac[h] = jnp.where(hit, wgt, 0.0).astype(BF)

    with jax.named_scope("wait_weights"):
        for copy in w_copies + s_copies:
            copy.wait()

    def ret_at(j, h, a):
        return j * 2 + h if a is None else 32 + ((j - 12) * 2 + h) * len(sums) + a

    def ret_cols(a):
        return pl.ds(0, full) if a is None else sums[a]

    def ret_copy(j, h, p, dc, a=None):
        here = rows(j * msg + h * half, half)
        there = rows((2 * p + c) * half, half)
        return pltpu.make_async_remote_copy(
            src_ref=stage.at[here, ret_cols(a)],
            dst_ref=ret.at[h, there, ret_cols(a)],
            send_sem=ret_send.at[ret_at(j, h, a)],
            recv_sem=ret_recv.at[ret_at(2 * p + c, h, a)],
            device_id=device(flipped(me, FLIPS[p], dc, outer), dc),
            device_id_type=MESH,
        )

    def ret_self(h):
        here = rows(c * msg + h * half, half)
        return pltpu.make_async_copy(stage.at[here], ret.at[h, rows(c * half, half)], l_sem.at[2 + h])

    def ret_arrival(j, h, a=None):
        return pltpu.make_async_remote_copy(
            src_ref=stage.at[rows(j * msg + h * half, half), ret_cols(a)],
            dst_ref=ret.at[h, rows(j * half, half), ret_cols(a)],
            send_sem=ret_send.at[ret_at(j, h, a)],
            recv_sem=ret_recv.at[ret_at(j, h, a)],
            device_id=device(me, 1 - c),
            device_id_type=MESH,
        )

    with jax.named_scope("wait_first"):
        dis_sent(0)
        for h in range(2):
            dis_start(h, 2)

    batch = 4 * msg
    elane = lax.broadcasted_iota(jnp.int32, (batch, ext), 1)
    for k in range(4):
        with jax.named_scope("permute_saved"):
            permute_saved(k)
        with jax.named_scope("wait_rows"):
            for j in range(4 * k, 4 * k + 4):
                if j >= 2:
                    for h in range(2):
                        dis_arrival(j, h).wait_recv()
            if k == 0:
                for h in range(2):
                    dis_arrival(1 - c, h).wait_recv()
                    dis_self(h).wait()
        buf = gb.at[pl.ds((k % 2) * batch, batch)]
        load = pltpu.make_async_copy(recv.at[pl.ds(k * batch, batch)], buf, l_sem.at[4])
        with jax.named_scope("load_rows"):
            load.start()
            load.wait()

        cacc[...] = jnp.zeros_like(cacc)
        tile = 256

        @pl.loop(0, hidden // tile)
        def _(n):
            cols = pl.ds(pl.multiple_of(n * tile, tile), tile)
            dh = lax.dot_general(buf[...], dw[cols, :], NT, preferred_element_type=F32)
            g, u = gf[:, cols].astype(F32), uf[:, cols].astype(F32)
            sg = jax.nn.sigmoid(g)
            a = g * sg
            prod = a * u * dh
            total = cacc[...]
            for b in range(tile // ext):
                total = total + prod[:, b * ext : (b + 1) * ext]
            cacc[...] = total
            dg[:, cols] = (dh * u * sg * (1.0 + g * (1.0 - sg))).astype(BF)
            du[:, cols] = (dh * a).astype(BF)

        with jax.named_scope("wait_stage"):
            if k == 0:
                dis_sent(1)
                for h in range(2):
                    dis_start(h, 3)
            elif k > 1:
                dis_sent(k)

        here = pl.ds(k * batch, batch)
        comb = jnp.sum(cacc[...], axis=1, keepdims=True)
        stage[here, width:full] = jnp.where(elane == my_expert, comb, 0.0).astype(BF)
        for a in range(len(sums)):
            cols = pl.ds(a * piece, min(piece, width - a * piece))
            x = lax.dot_general(dg[...], gw[cols, :], NT, preferred_element_type=F32)
            x = x + lax.dot_general(du[...], uw[cols, :], NT, preferred_element_type=F32)
            stage[here, cols] = x.astype(BF)
            if k == 3:
                for j in range(12, 16):
                    for h in range(2):
                        ret_copy(j, h, j // 2, j % 2, a).start()
        if k == 0:
            for h in range(2):
                ret_self(h).start()
                ret_copy(1 - c, h, 0, 1 - c).start()
        if k < 3:
            for j in range(max(4 * k, 2), 4 * k + 4):
                for h in range(2):
                    ret_copy(j, h, j // 2, j % 2).start()

    for a in range(3):
        for r in range(1, 8):
            tok_arrival(a, r).wait_send()

    def part_copy(a, r):
        stage_ = r.bit_length() - 1
        return pltpu.make_async_remote_copy(
            src_ref=tok.at[rows(member(relative(a, r)) * tokens, tokens), sums[a]],
            dst_ref=part.at[pl.ds(r * tokens, tokens), sums[a]],
            send_sem=part_send.at[a * 8 + r],
            recv_sem=part_recv.at[a * 8 + r],
            device_id=partner(a, stage_),
            device_id_type=MESH,
        )

    def combine_part(a):
        loads = []
        for h in range(2):
            loads.append(
                pltpu.make_async_copy(
                    ret.at[h, :, sums[a]], gb.at[:, pl.ds(h * piece, sums[a].size)], l_sem.at[5 + h]
                )
            )
        with jax.named_scope("load_returns"):
            for load in loads:
                load.start()
        for h, load in enumerate(loads):
            load.wait()
            there = pl.ds(h * 4 * tokens, 4 * tokens)
            size = min(piece, width - a * piece)
            got = gb[:, h * piece : h * piece + size]
            tok[there, a * piece : a * piece + size] = jnp.dot(
                wplac[h], got, preferred_element_type=F32
            ).astype(BF)
            if size < sums[a].size:
                got = gb[:, h * piece + size : h * piece + size + ext]
                tok[there, width:full] = jnp.dot(plac[h], got, preferred_element_type=F32).astype(BF)
        for r in range(4, 8):
            part_copy(a, r).start()

    def gathered(a, r, first):
        cols = sums[a]
        total = tok[rows(member(relative(a, r)) * tokens, tokens), cols].astype(F32)
        for stage_ in range(2, first - 1, -1):
            at = r + (1 << stage_)
            total = total + part[at * tokens : (at + 1) * tokens, cols].astype(F32)
        return total

    def pass_on(a, stage_):
        with jax.named_scope("wait_parts"):
            for r in range(1 << stage_, 2 << stage_):
                part_copy(a, r).wait_recv()
        if stage_ == 0:
            return
        for r in range(1 << (stage_ - 1), 1 << stage_):
            cols = sums[a]
            tok[rows(member(relative(a, r)) * tokens, tokens), cols] = gathered(a, r, stage_).astype(BF)
            part_copy(a, r).start()

    with jax.named_scope("wait_returns"):
        for h in range(2):
            for j in range(2, 12):
                ret_arrival(j, h).wait_recv()
            ret_arrival(1 - c, h).wait_recv()
            ret_self(h).wait()

    def wait_last(a):
        with jax.named_scope("wait_last"):
            for h in range(2):
                for j in range(12, 16):
                    ret_arrival(j, h, a).wait_recv()

    def finish(a):
        pass_on(a, 0)
        total = gathered(a, 0, 0)
        size = min(piece, width - a * piece)
        out_ref[:, a * piece : a * piece + size] = total[:, :size].astype(BF)
        return total

    count = len(sums)
    for a in range(count + 3):
        if a < count:
            wait_last(a)
            combine_part(a)
        if 1 <= a < count + 1:
            pass_on(a - 1, 2)
        if 2 <= a < count + 2:
            pass_on(a - 2, 1)
        if a >= 3:
            total = finish(a - 3)
    total = total[:, width % piece :]
    total = jnp.where(lane < 64, total, 0.0)
    same = jnp.where(iota((ext, ext), 0) == iota((ext, ext), 1), 1.0, 0.0).astype(BF)
    total_t = lax.dot_general(same, total.astype(BF), NT, preferred_element_type=F32)
    ksub = lax.broadcasted_iota(jnp.int32, ids.shape, 0)
    result = jnp.zeros(ids.shape, F32)
    for k in range(ids.shape[0]):
        value = jnp.sum(jnp.where(ids[k : k + 1, :] == sub, total_t, 0.0), axis=0, keepdims=True)
        result = jnp.where(ksub == k, value, result)
    outc_ref[...] = result.astype(BF)

    with jax.named_scope("wait_sends"):
        for a in range(count):
            for r in range(1, 8):
                part_copy(a, r).wait_send()
        for h in range(2):
            ret_copy(1 - c, h, 0, 1 - c).wait_send()
            for j in range(2, 12):
                ret_copy(j, h, j // 2, j % 2).wait_send()
            for j in range(12, 16):
                for a in range(count):
                    ret_copy(j, h, j // 2, j % 2, a).wait_send()


def body(grad_out, expert_ids, combine, gate_saved, up_saved, gate_weight, up_weight, down_weight):
    tokens, width = grad_out.shape
    sources, slots, hidden = gate_saved.shape
    top = expert_ids.shape[1]
    full = width + 128
    half = 4 * slots
    cover = 16 * half
    batch = 8 * half
    vmem = pl.BlockSpec(memory_space=pltpu.VMEM)
    hbm = pl.BlockSpec(memory_space=pl.ANY)
    dma = pltpu.SemaphoreType.DMA
    out = pl.pallas_call(
        functools.partial(kernel, tokens, slots, width, hidden),
        out_shape=(
            jax.ShapeDtypeStruct((tokens, width), BF),
            jax.ShapeDtypeStruct((top, tokens), BF),
            jax.ShapeDtypeStruct((2 * cover, width), BF),
            jax.ShapeDtypeStruct((2, cover, full), BF),
        ),
        in_specs=[vmem, vmem, vmem, hbm, hbm, hbm, hbm, hbm],
        out_specs=(vmem, vmem, hbm, hbm),
        scratch_shapes=[
            pltpu.VMEM((8 * tokens, full), BF),
            pltpu.VMEM((2 * cover, full), BF),
            pltpu.VMEM((width, hidden), BF),
            pltpu.VMEM((width, hidden), BF),
            pltpu.VMEM((hidden, width), BF),
            pltpu.VMEM((2 * cover, hidden), BF),
            pltpu.VMEM((2 * cover, hidden), BF),
            pltpu.VMEM((batch, hidden), BF),
            pltpu.VMEM((batch, hidden), BF),
            pltpu.VMEM((batch, hidden), BF),
            pltpu.VMEM((batch, hidden), BF),
            pltpu.VMEM((batch, 2 * cover), BF),
            pltpu.VMEM((batch, 128), F32),
            pltpu.VMEM((cover, width), BF),
            pltpu.VMEM((2, cover, 4 * tokens), BF),
            pltpu.VMEM((cover, 128), BF),
            pltpu.VMEM((cover, 128), BF),
            pltpu.VMEM((2, 4 * tokens, cover), BF),
            pltpu.VMEM((2, 4 * tokens, cover), BF),
            pltpu.VMEM((8 * tokens, full), BF),
            dma((5,)),
            dma((7,)),
            dma((24,)),
            dma((24,)),
            dma((32,)),
            dma((32,)),
            dma((32 + 48,)),
            dma((32 + 48,)),
            dma((48,)),
            dma((48,)),
        ],
        compiler_params=pltpu.CompilerParams(
            collective_id=0, has_side_effects=True, vmem_limit_bytes=66 * 1000 * 1000
        ),
        cost_estimate=pl.CostEstimate(
            flops=6 * sources * slots * hidden * width,
            bytes_accessed=80_000_000,
            transcendentals=sources * slots * hidden,
        ),
    )(
        grad_out,
        expert_ids.T,
        combine.T,
        gate_saved.transpose(1, 0, 2).reshape(2 * cover, hidden),
        up_saved.transpose(1, 0, 2).reshape(2 * cover, hidden),
        gate_weight,
        up_weight,
        down_weight,
    )
    return out[0], out[1].T


def solution(mesh):
    placed = (
        P(("ctx", "tp"), None),
        P(("ctx", "tp"), None),
        P(("ctx", "tp"), None),
        P(None, None, ("ctx", "tp")),
        P(None, None, ("ctx", "tp")),
        P(None, ("ctx", "tp")),
        P(None, ("ctx", "tp")),
        P(("ctx", "tp"), None),
    )
    return jax.shard_map(
        body,
        mesh=mesh,
        in_specs=placed,
        out_specs=(P(("ctx", "tp"), None), P(("ctx", "tp"), None)),
        check_vma=False,
    )
```

```python
import functools

import jax
import jax.numpy as jnp
from jax import lax
from jax.experimental import pallas as pl
from jax.experimental.pallas import tpu as pltpu
from jax.sharding import PartitionSpec as P

MESH = pl.DeviceIdType.MESH
FLIPS = (0, 7, 1, 6, 2, 5, 3, 4)
BF = jnp.bfloat16
F32 = jnp.float32
NT = (((1,), (1,)), ((), ()))


def bits(f):
    return f & 1, (f >> 1) & 1, (f >> 2) & 1


def outer(v, c):
    return (v + 3 + 2 * ((v + c) % 2)) % 4


def inner(v, c):
    return (v + 1 + 2 * ((v + c) % 2)) % 4


def flipped(xyz, f, c, how):
    return tuple(how(v, c) if b else v for v, b in zip(xyz, bits(f)))


def device(xyz, c):
    x, y, z = xyz
    return ((y // 2 * 4 + z) * 2 + c, (y % 2) * 4 + x)


def expert_of(xyz, c):
    ctx, tp = device(xyz, c)
    return ctx * 4 + tp // 2


def iota(shape, dim):
    return lax.broadcasted_iota(jnp.int32, shape, dim).astype(F32)


def kernel(
    tokens, slots, width, hidden,
    grad_ref, ids_ref, comb_ref, gate_hbm, up_hbm, gw_hbm, uw_hbm, dw_hbm,
    out_ref, outc_ref, recv, ret,
    tok, stage, gw, uw, dw, sav_g, sav_u, gf, uf, dg, du, perm, cacc, gb, sel, selp, selw, plac, wplac, part,
    w_sem, l_sem, tok_send, tok_recv, dis_send, dis_recv, ret_send, ret_recv, part_send, part_recv,
):
    ext = 128
    full = width + ext
    half = 4 * slots
    msg = 2 * half
    cover = 16 * half
    ctx, tp = lax.axis_index("ctx"), lax.axis_index("tp")
    c = ctx % 2
    me = (tp % 4, ctx // 8 * 2 + tp // 4, ctx // 2 % 4)
    mbit = tuple((v + c) % 2 for v in me)
    mine = mbit[2] * 4 + mbit[1] * 2 + mbit[0]
    my_expert = expert_of(me, c)

    def member(r):
        b = tuple(1 - v if t else v for v, t in zip(mbit, bits(r)))
        return b[2] * 4 + b[1] * 2 + b[0]

    def rows(start, size):
        return pl.ds(pl.multiple_of(start, 16), size)

    w_copies = [
        pltpu.make_async_copy(a, b, w_sem.at[i])
        for i, (a, b) in enumerate(((dw_hbm, dw), (gw_hbm, gw), (uw_hbm, uw)))
    ]
    for copy in w_copies:
        copy.start()

    s_copies = [
        pltpu.make_async_copy(a, b, w_sem.at[3 + i])
        for i, (a, b) in enumerate(((gate_hbm, sav_g), (up_hbm, sav_u)))
    ]
    for copy in s_copies:
        copy.start()

    def source_parts(sender, sc):
        out = []
        for v, part_of in zip(
            sender, (lambda x: x, lambda y: y // 2 * 64 + y % 2 * 4, lambda z: z * 16)
        ):
            low = v - (v + sc) % 2 + 4
            out.append((part_of(low % 4), part_of((low + 1) % 4)))
        return out

    def permute_saved(k):
        r = iota((msg, 1), 0)
        m = jnp.floor((r + 0.5) * (1.0 / slots))
        slot = r - m * slots
        mz = jnp.floor((m + 0.5) * 0.25)
        my = jnp.floor((m - 4 * mz + 0.5) * 0.5)
        mx = m - 4 * mz - 2 * my
        lanes = iota((1, cover * 2), 1)
        for q in range(4):
            p, sc = 2 * k + q // 2, q % 2
            parts = source_parts(flipped(me, FLIPS[p], sc, outer), sc)
            at = slot * (cover * 2 // slots) + 8.0 * sc
            for bit, (low, high) in zip((mx, my, mz), parts):
                at = at + jnp.where(bit > 0.5, high.astype(F32), low.astype(F32))
            perm[q * msg : (q + 1) * msg, :] = jnp.where(at == lanes, 1.0, 0.0).astype(BF)
        for src, dst in ((sav_g, gf), (sav_u, uf)):
            for n in range(hidden // 256):
                cols = slice(n * 256, (n + 1) * 256)
                dst[:, cols] = jnp.dot(perm[...], src[:, cols], preferred_element_type=F32).astype(BF)

    barrier = pltpu.get_barrier_semaphore()
    friends = [device(me, 1 - c)]
    for f in range(1, 8):
        friends.append(device(flipped(me, f, c, outer), c))
        friends.append(device(flipped(me, f, c, outer), 1 - c))
        friends.append(device(flipped(me, f, 1 - c, outer), 1 - c))
        friends.append(device(flipped(me, f, c, inner), c))
    for friend in friends:
        pl.semaphore_signal(barrier, inc=1, device_id=friend, device_id_type=MESH)

    own = rows(mine * tokens, tokens)
    tok[own, 0:width] = grad_ref[...]
    sub = lax.broadcasted_iota(jnp.int32, (ext, tokens), 0)
    sub64 = jnp.where(sub >= 64, sub - 64, sub)
    ids = ids_ref[...]
    combine = comb_ref[...].astype(F32)
    hot_t = jnp.zeros((ext, tokens), F32)
    weight_t = jnp.zeros((ext, tokens), F32)
    for k in range(ids.shape[0]):
        same = ids[k : k + 1, :] == sub64
        hot_t = jnp.where(same, 1.0, hot_t)
        weight_t = jnp.where(same, combine[k : k + 1, :], weight_t)
    row, col = iota((tokens, tokens), 0), iota((tokens, tokens), 1)
    lower = jnp.where(col < row, 1.0, 0.0).astype(BF)
    same = jnp.where(col == row, 1.0, 0.0).astype(BF)
    count = lax.dot_general(lower, hot_t.astype(BF), NT, preferred_element_type=F32)
    hot = lax.dot_general(same, hot_t.astype(BF), NT, preferred_element_type=F32)
    weight = lax.dot_general(same, weight_t.astype(BF), NT, preferred_element_type=F32)
    lane = lax.broadcasted_iota(jnp.int32, (tokens, ext), 1)
    table = jnp.where(lane < 64, jnp.where(hot > 0.5, count, -1.0), weight)
    tok[own, width:full] = table.astype(BF)

    with jax.named_scope("barrier"):
        pl.semaphore_wait(barrier, len(friends))

    third = full // 3
    parts = [pl.ds(a * third, third) for a in range(3)]
    piece = 6 * ext
    sums = [pl.ds(a * piece, min(piece, full - a * piece)) for a in range(-(-full // piece))]

    def relative(a, r):
        return sum(((r >> i) & 1) << ((a + i) % 3) for i in range(3))

    def partner(a, stage_):
        return device(flipped(me, 1 << ((a + stage_) % 3), c, inner), c)

    def tok_copy(a, r, stage_):
        block = tok.at[rows(member(relative(a, r)) * tokens, tokens), parts[a]]
        return pltpu.make_async_remote_copy(
            src_ref=block,
            dst_ref=block,
            send_sem=tok_send.at[a * 8 + r + (1 << stage_)],
            recv_sem=tok_recv.at[a * 8 + r + (1 << stage_)],
            device_id=partner(a, stage_),
            device_id_type=MESH,
        )

    def tok_arrival(a, r):
        stage_ = r.bit_length() - 1
        block = tok.at[rows(member(relative(a, r)) * tokens, tokens), parts[a]]
        return pltpu.make_async_remote_copy(
            src_ref=block,
            dst_ref=block,
            send_sem=tok_send.at[a * 8 + r],
            recv_sem=tok_recv.at[a * 8 + r],
            device_id=partner(a, stage_),
            device_id_type=MESH,
        )

    for stage_ in range(3):
        for a in range(3):
            tok_copy(a, 0, stage_).start()

    slane = lax.broadcasted_iota(jnp.int32, (half, ext), 1)
    for i in range(16):
        e = expert_of(flipped(me, FLIPS[i // 2], c, outer), i % 2)
        selp[i * half : (i + 1) * half, :] = jnp.where(slane == e, 1.0, 0.0).astype(BF)
        selw[i * half : (i + 1) * half, :] = jnp.where(slane == e + 64, 1.0, 0.0).astype(BF)

    def slot_of(j):
        block = jnp.floor((j + 0.5) * (1.0 / slots))
        group = jnp.floor((block + 0.5) * 0.25)
        return j - block * slots, block - group * 4

    def owner_of(t):
        return jnp.floor((t + 0.5) * (1.0 / tokens))

    def dis_copy(i, h, p, dc):
        here = rows(i * msg + h * half, half)
        there = rows((2 * p + c) * msg + h * half, half)
        dst = device(flipped(me, FLIPS[p], c, outer), dc)
        return pltpu.make_async_remote_copy(
            src_ref=stage.at[here, pl.ds(0, width)],
            dst_ref=recv.at[there],
            send_sem=dis_send.at[i * 2 + h],
            recv_sem=dis_recv.at[(2 * p + c) * 2 + h],
            device_id=dst,
            device_id_type=MESH,
        )

    def dis_self(h):
        here = rows(c * msg + h * half, half)
        return pltpu.make_async_copy(stage.at[here, pl.ds(0, width)], recv.at[here], l_sem.at[h])

    def dis_arrival(j, h):
        here = rows(j * msg + h * half, half)
        return pltpu.make_async_remote_copy(
            src_ref=stage.at[here, pl.ds(0, width)],
            dst_ref=recv.at[here],
            send_sem=dis_send.at[j * 2 + h],
            recv_sem=dis_recv.at[j * 2 + h],
            device_id=device(me, 1 - c),
            device_id_type=MESH,
        )

    def messages(k):
        return [(p, dc) for dc in (c, 1 - c) for p in (2 * k, 2 * k + 1) if p > 0]

    def dis_start(h, k):
        if k == 0:
            dis_self(h).start()
            dis_copy(1 - c, h, 0, 1 - c).start()
        for p, dc in messages(k):
            dis_copy(2 * p + dc, h, p, dc).start()

    def dis_sent(k):
        if k == 0:
            for h in range(2):
                dis_copy(1 - c, h, 0, 1 - c).wait_send()
        for j in range(max(4 * k, 2), 4 * k + 4):
            for h in range(2):
                dis_copy(j, h, j // 2, j % 2).wait_send()

    def select(step, h, later):
        there = rows(h * 4 * tokens, 4 * tokens)
        size = cover // 2
        tile = 512

        @pl.loop(0, width // tile)
        def _(n):
            cols = pl.ds(pl.multiple_of(n * tile, tile), tile)
            chosen = sel[step, later * size : (later + 1) * size]
            got = jnp.dot(chosen, tok[there, cols], preferred_element_type=F32).astype(BF)
            for i in range(8):
                stage[rows((8 * later + i) * msg + h * half, half), cols] = got[i * half : (i + 1) * half]

    with jax.named_scope("forward_tokens"):
        for r in range(1, 4):
            for a in range(3):
                tok_arrival(a, r).wait_recv()
                for stage_ in range(r.bit_length(), 3):
                    tok_copy(a, r, stage_).start()

    for step in range(2):
        h = mbit[2] if step == 0 else 1 - mbit[2]
        with jax.named_scope("wait_tokens"):
            for r in range(4, 8):
                for a in range(3):
                    if (relative(a, r) >> 2) == step:
                        tok_arrival(a, r).wait_recv()
        there = rows(h * 4 * tokens, 4 * tokens)
        tables = tok[there, width:full]
        pos = lax.dot_general(selp[...], tables, NT, preferred_element_type=F32)
        slot, four = slot_of(iota((cover, 1), 0))
        owner = owner_of(iota((1, 4 * tokens), 1))
        sel[step] = jnp.where((pos == slot) & (four == owner), 1.0, 0.0).astype(BF)

        select(step, h, 0)
        dis_start(h, 0)
        dis_start(h, 1)

    for step in range(2):
        h = mbit[2] if step == 0 else 1 - mbit[2]
        select(step, h, 1)
        dis_start(h, 2)

    slot, four = slot_of(iota((1, cover), 1))
    owner = owner_of(iota((4 * tokens, 1), 0))
    for h in range(2):
        tables = tok[h * 4 * tokens : (h + 1) * 4 * tokens, width:full]
        pos = lax.dot_general(tables, selp[...], NT, preferred_element_type=F32)
        wgt = lax.dot_general(tables, selw[...], NT, preferred_element_type=F32)
        hit = (pos == slot) & (four == owner)
        plac[h] = jnp.where(hit, 1.0, 0.0).astype(BF)
        wplac[h] = jnp.where(hit, wgt, 0.0).astype(BF)

    with jax.named_scope("wait_weights"):
        for copy in w_copies + s_copies:
            copy.wait()

    def ret_at(j, h, a):
        return j * 2 + h if a is None else 32 + ((j - 8) * 2 + h) * len(sums) + a

    def ret_cols(a):
        return pl.ds(0, full) if a is None else sums[a]

    def ret_copy(j, h, p, dc, a=None):
        here = rows(j * msg + h * half, half)
        there = rows((2 * p + c) * half, half)
        return pltpu.make_async_remote_copy(
            src_ref=stage.at[here, ret_cols(a)],
            dst_ref=ret.at[h, there, ret_cols(a)],
            send_sem=ret_send.at[ret_at(j, h, a)],
            recv_sem=ret_recv.at[ret_at(2 * p + c, h, a)],
            device_id=device(flipped(me, FLIPS[p], dc, outer), dc),
            device_id_type=MESH,
        )

    def ret_self(h):
        here = rows(c * msg + h * half, half)
        return pltpu.make_async_copy(stage.at[here], ret.at[h, rows(c * half, half)], l_sem.at[2 + h])

    def ret_arrival(j, h, a=None):
        return pltpu.make_async_remote_copy(
            src_ref=stage.at[rows(j * msg + h * half, half), ret_cols(a)],
            dst_ref=ret.at[h, rows(j * half, half), ret_cols(a)],
            send_sem=ret_send.at[ret_at(j, h, a)],
            recv_sem=ret_recv.at[ret_at(j, h, a)],
            device_id=device(me, 1 - c),
            device_id_type=MESH,
        )

    with jax.named_scope("wait_first"):
        dis_sent(0)
        for h in range(2):
            dis_start(h, 3)

    def ret_part(k, a):
        for p, dc in messages(k):
            for h in range(2):
                ret_copy(2 * p + dc, h, p, dc, a).start()

    batch = 4 * msg
    elane = lax.broadcasted_iota(jnp.int32, (batch, ext), 1)
    for k in range(4):
        with jax.named_scope("permute_saved"):
            permute_saved(k)
        with jax.named_scope("wait_rows"):
            for j in range(4 * k, 4 * k + 4):
                if j >= 2:
                    for h in range(2):
                        dis_arrival(j, h).wait_recv()
            if k == 0:
                for h in range(2):
                    dis_arrival(1 - c, h).wait_recv()
                    dis_self(h).wait()
        buf = gb.at[pl.ds((k % 2) * batch, batch)]
        load = pltpu.make_async_copy(recv.at[pl.ds(k * batch, batch)], buf, l_sem.at[4])
        with jax.named_scope("load_rows"):
            load.start()
            load.wait()

        cacc[...] = jnp.zeros_like(cacc)
        tile = 256

        @pl.loop(0, hidden // tile)
        def _(n):
            cols = pl.ds(pl.multiple_of(n * tile, tile), tile)
            dh = lax.dot_general(buf[...], dw[cols, :], NT, preferred_element_type=F32)
            g, u = gf[:, cols].astype(F32), uf[:, cols].astype(F32)
            sg = jax.nn.sigmoid(g)
            a = g * sg
            prod = a * u * dh
            total = cacc[...]
            for b in range(tile // ext):
                total = total + prod[:, b * ext : (b + 1) * ext]
            cacc[...] = total
            dg[:, cols] = (dh * u * sg * (1.0 + g * (1.0 - sg))).astype(BF)
            du[:, cols] = (dh * a).astype(BF)

        with jax.named_scope("wait_stage"):
            if k > 0:
                dis_sent(k)

        here = pl.ds(k * batch, batch)
        comb = jnp.sum(cacc[...], axis=1, keepdims=True)
        stage[here, width:full] = jnp.where(elane == my_expert, comb, 0.0).astype(BF)
        for a in range(len(sums)):
            cols = pl.ds(a * piece, min(piece, width - a * piece))
            x = lax.dot_general(dg[...], gw[cols, :], NT, preferred_element_type=F32)
            x = x + lax.dot_general(du[...], uw[cols, :], NT, preferred_element_type=F32)
            stage[here, cols] = x.astype(BF)
            if k >= 2 and a < len(sums) // 2:
                ret_part(k, a)
        if k == 3:
            for a in range(len(sums) // 2, len(sums)):
                for b in (2, 3):
                    ret_part(b, a)
        if k == 0:
            for h in range(2):
                ret_self(h).start()
                ret_copy(1 - c, h, 0, 1 - c).start()
        if k < 2:
            for p, dc in messages(k):
                for h in range(2):
                    ret_copy(2 * p + dc, h, p, dc).start()

    for a in range(3):
        for r in range(1, 8):
            tok_arrival(a, r).wait_send()

    def part_copy(a, r):
        stage_ = r.bit_length() - 1
        return pltpu.make_async_remote_copy(
            src_ref=tok.at[rows(member(relative(a, r)) * tokens, tokens), sums[a]],
            dst_ref=part.at[pl.ds(r * tokens, tokens), sums[a]],
            send_sem=part_send.at[a * 8 + r],
            recv_sem=part_recv.at[a * 8 + r],
            device_id=partner(a, stage_),
            device_id_type=MESH,
        )

    def combine_part(a):
        loads = []
        for h in range(2):
            loads.append(
                pltpu.make_async_copy(
                    ret.at[h, :, sums[a]], gb.at[:, pl.ds(h * piece, sums[a].size)], l_sem.at[5 + h]
                )
            )
        with jax.named_scope("load_returns"):
            for load in loads:
                load.start()
        for h, load in enumerate(loads):
            load.wait()
            there = pl.ds(h * 4 * tokens, 4 * tokens)
            size = min(piece, width - a * piece)
            got = gb[:, h * piece : h * piece + size]
            tok[there, a * piece : a * piece + size] = jnp.dot(
                wplac[h], got, preferred_element_type=F32
            ).astype(BF)
            if size < sums[a].size:
                got = gb[:, h * piece + size : h * piece + size + ext]
                tok[there, width:full] = jnp.dot(plac[h], got, preferred_element_type=F32).astype(BF)
        for r in range(4, 8):
            part_copy(a, r).start()

    def gathered(a, r, first):
        cols = sums[a]
        total = tok[rows(member(relative(a, r)) * tokens, tokens), cols].astype(F32)
        for stage_ in range(2, first - 1, -1):
            at = r + (1 << stage_)
            total = total + part[at * tokens : (at + 1) * tokens, cols].astype(F32)
        return total

    def pass_on(a, stage_):
        with jax.named_scope("wait_parts"):
            for r in range(1 << stage_, 2 << stage_):
                part_copy(a, r).wait_recv()
        if stage_ == 0:
            return
        for r in range(1 << (stage_ - 1), 1 << stage_):
            cols = sums[a]
            tok[rows(member(relative(a, r)) * tokens, tokens), cols] = gathered(a, r, stage_).astype(BF)
            part_copy(a, r).start()

    with jax.named_scope("wait_returns"):
        for h in range(2):
            for j in range(2, 8):
                ret_arrival(j, h).wait_recv()
            ret_arrival(1 - c, h).wait_recv()
            ret_self(h).wait()

    def wait_last(a):
        with jax.named_scope("wait_last"):
            for h in range(2):
                for j in range(8, 16):
                    ret_arrival(j, h, a).wait_recv()

    def finish(a):
        pass_on(a, 0)
        total = gathered(a, 0, 0)
        size = min(piece, width - a * piece)
        out_ref[:, a * piece : a * piece + size] = total[:, :size].astype(BF)
        return total

    count = len(sums)
    for a in range(count + 3):
        if a < count:
            wait_last(a)
            combine_part(a)
        if 1 <= a < count + 1:
            pass_on(a - 1, 2)
        if 2 <= a < count + 2:
            pass_on(a - 2, 1)
        if a >= 3:
            total = finish(a - 3)
    total = total[:, width % piece :]
    total = jnp.where(lane < 64, total, 0.0)
    same = jnp.where(iota((ext, ext), 0) == iota((ext, ext), 1), 1.0, 0.0).astype(BF)
    total_t = lax.dot_general(same, total.astype(BF), NT, preferred_element_type=F32)
    ksub = lax.broadcasted_iota(jnp.int32, ids.shape, 0)
    result = jnp.zeros(ids.shape, F32)
    for k in range(ids.shape[0]):
        value = jnp.sum(jnp.where(ids[k : k + 1, :] == sub, total_t, 0.0), axis=0, keepdims=True)
        result = jnp.where(ksub == k, value, result)
    outc_ref[...] = result.astype(BF)

    with jax.named_scope("wait_sends"):
        for a in range(count):
            for r in range(1, 8):
                part_copy(a, r).wait_send()
        for h in range(2):
            ret_copy(1 - c, h, 0, 1 - c).wait_send()
            for j in range(2, 8):
                ret_copy(j, h, j // 2, j % 2).wait_send()
            for j in range(8, 16):
                for a in range(count):
                    ret_copy(j, h, j // 2, j % 2, a).wait_send()


def body(grad_out, expert_ids, combine, gate_saved, up_saved, gate_weight, up_weight, down_weight):
    tokens, width = grad_out.shape
    sources, slots, hidden = gate_saved.shape
    top = expert_ids.shape[1]
    full = width + 128
    half = 4 * slots
    cover = 16 * half
    batch = 8 * half
    vmem = pl.BlockSpec(memory_space=pltpu.VMEM)
    hbm = pl.BlockSpec(memory_space=pl.ANY)
    dma = pltpu.SemaphoreType.DMA
    out = pl.pallas_call(
        functools.partial(kernel, tokens, slots, width, hidden),
        out_shape=(
            jax.ShapeDtypeStruct((tokens, width), BF),
            jax.ShapeDtypeStruct((top, tokens), BF),
            jax.ShapeDtypeStruct((2 * cover, width), BF),
            jax.ShapeDtypeStruct((2, cover, full), BF),
        ),
        in_specs=[vmem, vmem, vmem, hbm, hbm, hbm, hbm, hbm],
        out_specs=(vmem, vmem, hbm, hbm),
        scratch_shapes=[
            pltpu.VMEM((8 * tokens, full), BF),
            pltpu.VMEM((2 * cover, full), BF),
            pltpu.VMEM((width, hidden), BF),
            pltpu.VMEM((width, hidden), BF),
            pltpu.VMEM((hidden, width), BF),
            pltpu.VMEM((2 * cover, hidden), BF),
            pltpu.VMEM((2 * cover, hidden), BF),
            pltpu.VMEM((batch, hidden), BF),
            pltpu.VMEM((batch, hidden), BF),
            pltpu.VMEM((batch, hidden), BF),
            pltpu.VMEM((batch, hidden), BF),
            pltpu.VMEM((batch, 2 * cover), BF),
            pltpu.VMEM((batch, 128), F32),
            pltpu.VMEM((cover, width), BF),
            pltpu.VMEM((2, cover, 4 * tokens), BF),
            pltpu.VMEM((cover, 128), BF),
            pltpu.VMEM((cover, 128), BF),
            pltpu.VMEM((2, 4 * tokens, cover), BF),
            pltpu.VMEM((2, 4 * tokens, cover), BF),
            pltpu.VMEM((8 * tokens, full), BF),
            dma((5,)),
            dma((7,)),
            dma((24,)),
            dma((24,)),
            dma((32,)),
            dma((32,)),
            dma((32 + 96,)),
            dma((32 + 96,)),
            dma((48,)),
            dma((48,)),
        ],
        compiler_params=pltpu.CompilerParams(
            collective_id=0, has_side_effects=True, vmem_limit_bytes=66 * 1000 * 1000
        ),
        cost_estimate=pl.CostEstimate(
            flops=6 * sources * slots * hidden * width,
            bytes_accessed=80_000_000,
            transcendentals=sources * slots * hidden,
        ),
    )(
        grad_out,
        expert_ids.T,
        combine.T,
        gate_saved.transpose(1, 0, 2).reshape(2 * cover, hidden),
        up_saved.transpose(1, 0, 2).reshape(2 * cover, hidden),
        gate_weight,
        up_weight,
        down_weight,
    )
    return out[0], out[1].T


def solution(mesh):
    placed = (
        P(("ctx", "tp"), None),
        P(("ctx", "tp"), None),
        P(("ctx", "tp"), None),
        P(None, None, ("ctx", "tp")),
        P(None, None, ("ctx", "tp")),
        P(None, ("ctx", "tp")),
        P(None, ("ctx", "tp")),
        P(("ctx", "tp"), None),
    )
    return jax.shard_map(
        body,
        mesh=mesh,
        in_specs=placed,
        out_specs=(P(("ctx", "tp"), None), P(("ctx", "tp"), None)),
        check_vma=False,
    )
```
